512 devices in a mesh: gx: 32 (over y, x, core), gy: 16 (over z).
Axes of the slice: x: 4, y: 4, z: 16, core: 2. Of those that a mesh axis runs over, the one named last changes fastest.
Arguments:
- right_side: float32 [3, 512, 256, 512], P(None, 'gx', 'gy'), may hold values from -8 to 8
- viscosity: float32 [512, 256, 512], P('gx', 'gy'), may hold values from 0.05 to 20
- reaction: float32 [512, 256, 512], P('gx', 'gy'), may hold values from 0.5 to 4
- agg_ids: int32 [512, 256, 512], P('gx', 'gy'), may hold values from 0 to 511
- owner_map: int32 [32, 16], P('gx', 'gy'), may hold values from 0 to 31, as said below
Outputs:
- velocity: float32 [3, 512, 256, 512], P(None, 'gx', 'gy')
- corrections: float32 [32, 16, 4, 3, 512], P('gx', 'gy')
The draws below stay inside these ranges and needn't reach their ends.
Inputs may be any that keep to these rules, and one draw needn't show every extreme that they name: `owner_map`: in every column along gy exactly one owner takes the blocks of 4 devices, its own among them; 3 devices own no block; every other device owns its own block.
All inputs are finite; a program needn't handle non-finite values.
Results may differ from the reference program's by a relative error of at most 0.0003.
Values sent between devices are 32-bit elements; how exact they have to be, the bound alone decides.
No kernel may reach another device: no remote copies, remote signals or barrier semaphores. Data moves between devices by JAX's collectives and lax.ppermute only.
A program may use at most 64 MiB of HBM per device.

```python
import math
import jax
import jax.numpy as jnp
from jax import lax

CX = 16
CY = 16
CZ = 512
COMP = 3
NAGG = 512
NU = 3
MERGES = 3
MAXB = 4
NX = 512
NY = 256
NZ = 512
N_GX = 32
N_GY = 16


def draw_owner_map(key, part):
    key = jax.random.fold_in(key, 11)
    column_keys = jax.random.split(key, N_GY)
    ranks = jnp.arange(N_GX, dtype=jnp.int32)

    def one_column(column_key):
        order = jax.random.permutation(column_key, N_GX).astype(jnp.int32)
        target = jnp.where(ranks < MAXB, order[0], order)
        return jnp.zeros((N_GX,), jnp.int32).at[order].set(target)
    return jax.vmap(one_column)(column_keys).T


def place_ends(result, rng, low, largest):
    extent = result.shape
    index_at = [jax.random.randint(jax.random.fold_in(rng, axis), (), 0, extent[axis]) for axis in range(len(extent))]
    result = result.at[tuple(index_at)].set(low)
    longest = extent.index(max(extent))
    index_at[longest] = (index_at[longest] + 1) % extent[longest]
    return result.at[tuple(index_at)].set(largest)


def block_scale(stream_key, shape, pieces, smallest, top_value):
    factor_of, own = 1.0, jax.random.fold_in(stream_key, 6)
    for axis_at, parts in pieces:
        draws = jnp.exp(jax.random.uniform(jax.random.fold_in(own, axis_at), (parts,), jnp.float32, smallest / len(pieces), top_value / len(pieces)))
        factor_of = factor_of * jnp.repeat(draws, shape[axis_at] // parts).reshape([-1 if axis == axis_at else 1 for axis in range(len(shape))])
    return factor_of


def bell_draw(rng, dims, deviation, reach, pieces=(), kind=jnp.bfloat16):
    loudness = block_scale(rng, dims, pieces, -0.22, 0.18) if pieces else 1.0
    values = jax.random.normal(rng, dims, jnp.float32) * deviation * loudness
    return jnp.minimum(jnp.maximum(values, -reach), reach).astype(kind)


def setup_inputs(seed: int = 0) -> dict:
    seeds = jax.random.split(jax.random.key(seed), 6)
    return {
        "right_side": bell_draw(seeds[0], (COMP, NX, NY, NZ), 1.0, 8.0, ((1, 32), (2, 16)), jnp.float32),
        "viscosity": jnp.clip(jnp.exp(math.log(20.0) - 5.9914645 * jax.random.uniform(seeds[1], (NX, NY, NZ), jnp.float32) ** block_scale(seeds[1], (NX, NY, NZ), ((0, 32), (1, 16)), -0.2, 0.2)), 0.05, 20.0),
        "reaction": jnp.clip(jnp.exp(math.log(4.0) - 2.0794415 * jax.random.uniform(seeds[2], (NX, NY, NZ), jnp.float32) ** block_scale(seeds[2], (NX, NY, NZ), ((0, 32), (1, 16)), -0.2, 0.2)), 0.5, 4.0),
        "agg_ids": place_ends(jax.random.randint(seeds[3], (NX, NY, NZ), 0, NAGG), jax.random.fold_in(seeds[3], 1), 0, NAGG - 1).astype(jnp.int32),
        "owner_map": draw_owner_map(jax.random.fold_in(seeds[5], 71), 0),
    }


def face_weights(viscosity, reaction):
    padded_visc = jnp.pad(viscosity, 1)
    shifted = [padded_visc[2:, 1:-1, 1:-1], padded_visc[:-2, 1:-1, 1:-1], padded_visc[1:-1, 2:, 1:-1],
               padded_visc[1:-1, :-2, 1:-1], padded_visc[1:-1, 1:-1, 2:], padded_visc[1:-1, 1:-1, :-2]]
    weights = [0.5 * (viscosity + other) for other in shifted]
    diagonal = reaction + weights[0] + weights[1] + weights[2] + weights[3] + weights[4] + weights[5]
    return weights, diagonal


def apply_fine(padded_vel, field, weights, diagonal):
    beside = weights[0] * padded_vel[:, 2:, 1:-1, 1:-1] + weights[1] * padded_vel[:, :-2, 1:-1, 1:-1]
    beside = beside + weights[2] * padded_vel[:, 1:-1, 2:, 1:-1] + weights[3] * padded_vel[:, 1:-1, :-2, 1:-1]
    beside = beside + weights[4] * padded_vel[:, 1:-1, 1:-1, 2:] + weights[5] * padded_vel[:, 1:-1, 1:-1, :-2]
    return diagonal * field - beside


def coarse_apply(vector, coarse_diag):
    coupling = 0.2 * jnp.minimum(coarse_diag[..., :-1], coarse_diag[..., 1:])
    coupling = jnp.expand_dims(coupling, -2)
    zeros_end = jnp.zeros_like(vector[..., :1])
    upper = jnp.concatenate([coupling * vector[..., 1:], zeros_end], axis=-1)
    lower = jnp.concatenate([zeros_end, coupling * vector[..., :-1]], axis=-1)
    return jnp.expand_dims(coarse_diag, -2) * vector - (upper + lower)


def partner_rows(array, stride):
    count = array.shape[0]
    grouped = array.reshape((count // (2 * stride), 2, stride) + array.shape[1:])
    return grouped[:, ::-1].reshape(array.shape)


def all_levels(resid, coarse_diag):
    outputs = []
    for level in range(MERGES + 1):
        scaled = jnp.expand_dims(coarse_diag, -2)
        correction = 0.8 * resid / scaled
        correction = correction + 0.8 * (resid - coarse_apply(correction, coarse_diag)) / scaled
        outputs.append(correction)
        if level < MERGES:
            left_over = resid - coarse_apply(correction, coarse_diag)
            resid = left_over + partner_rows(left_over, 2 ** level)
            coarse_diag = coarse_diag + partner_rows(coarse_diag, 2 ** level)
    return outputs


def reference(right_side, viscosity, reaction, agg_ids, owner_map):
    weights, diagonal = face_weights(viscosity, reaction)
    widths = ((0, 0), (1, 1), (1, 1), (1, 1))
    velocity = jnp.zeros_like(right_side)
    for sweep in range(NU):
        image = apply_fine(jnp.pad(velocity, widths), velocity, weights, diagonal)
        velocity = velocity + 0.8 * (right_side - image) / diagonal
    resid = right_side - apply_fine(jnp.pad(velocity, widths), velocity, weights, diagonal)
    cells = CX * CY * CZ
    stacked = jnp.concatenate([resid, diagonal[None]], axis=0)
    stacked = stacked.reshape(COMP + 1, N_GX, CX, N_GY, CY, CZ).transpose(1, 3, 2, 4, 5, 0)
    stacked = stacked.reshape(N_GX * N_GY * cells, COMP + 1)
    local_ids = agg_ids.reshape(N_GX, CX, N_GY, CY, CZ).transpose(0, 2, 1, 3, 4).reshape(N_GX * N_GY, cells)
    block_base = (jnp.arange(N_GX * N_GY, dtype=jnp.int32) * NAGG)[:, None]
    global_ids = (local_ids + block_base).reshape(-1)
    block_sums = jax.ops.segment_sum(stacked, global_ids, num_segments=N_GX * N_GY * NAGG)
    block_sums = block_sums.reshape(N_GX, N_GY, NAGG, COMP + 1).transpose(0, 1, 3, 2)
    one_hot = (owner_map[:, :, None] == jnp.arange(N_GX, dtype=jnp.int32)[None, None, :]).astype(jnp.float32)
    owned = jnp.einsum('ijo,ijcn->ojcn', one_hot, block_sums, precision=lax.Precision.HIGHEST)
    outputs = all_levels(owned[:, :, :COMP], 1.0 + owned[:, :, COMP])
    return velocity, jnp.stack(outputs, axis=2)
```

```python
import jax
import jax.numpy as jnp
from jax import lax
from jax.experimental import pallas as pl
from jax.experimental.pallas import tpu as pltpu
from jax.sharding import PartitionSpec as P

COMP = 3
NAGG = 512
MERGES = 3
GROUP = 2**MERGES
LANES = 128
WIDE = 3
VWIDE = WIDE + 1
VISC_AT = COMP * WIDE
REACT_AT = VISC_AT + VWIDE
ROWS = REACT_AT + WIDE
X0 = 4
Y0 = 8
F32 = jnp.float32
BIG = 56 * 2**20


def pack_faces(rhs, visc, react, x_low, x_high, y_low, y_high):
    nx, ny, _ = visc.shape
    for c in range(COMP):
        for k in range(WIDE):
            x_low[c * WIDE + k] = rhs[c, k]
            x_high[c * WIDE + k] = rhs[c, nx - WIDE + k]
    for k in range(VWIDE):
        x_low[VISC_AT + k] = visc[k]
        x_high[VISC_AT + k] = visc[nx - VWIDE + k]
    for k in range(WIDE):
        x_low[REACT_AT + k] = react[k]
        x_high[REACT_AT + k] = react[nx - WIDE + k]
    for x in range(nx):
        for c in range(COMP):
            rows = pl.ds(c * WIDE, WIDE)
            y_low[x, rows] = rhs[c, x, pl.ds(0, WIDE)]
            y_high[x, rows] = rhs[c, x, pl.ds(ny - WIDE, WIDE)]
        rows = pl.ds(VISC_AT, VWIDE)
        y_low[x, rows] = visc[x, pl.ds(0, VWIDE)]
        y_high[x, rows] = visc[x, pl.ds(ny - VWIDE, VWIDE)]
        rows = pl.ds(REACT_AT, WIDE)
        y_low[x, rows] = react[x, pl.ds(0, WIDE)]
        y_high[x, rows] = react[x, pl.ds(ny - WIDE, WIDE)]


def corner_rows():
    table = []
    for away, at in ((1, 0), (2, 16), (3, 22)):
        left = WIDE - away
        if left:
            for c in range(COMP):
                table.append((away, "rhs", c, at, left))
                at += left
        table.append((away, "visc", 0, at, left + 1))
        at += left + 1
        if left:
            table.append((away, "react", 0, at, left))
    return table


def halo_index(side, away, kind, c):
    width = VWIDE if kind == "visc" else WIDE
    place = width - away if side == 0 else away - 1
    return {"rhs": c * WIDE, "visc": VISC_AT, "react": REACT_AT}[kind] + place


def pack_corners(from_low, from_high, y_low, y_high):
    ny = from_low.shape[1]
    for side, source in enumerate((from_low, from_high)):
        for away, kind, c, at, count in corner_rows():
            index = halo_index(side, away, kind, c)
            y_low[side, pl.ds(at, count)] = source[index, pl.ds(0, count)]
            y_high[side, pl.ds(at, count)] = source[index, pl.ds(ny - count, count)]


def chunks_of(value):
    return [value[..., c * LANES : (c + 1) * LANES] for c in range(value.shape[-1] // LANES)]


def z_up(parts):
    lane = lax.broadcasted_iota(jnp.int32, parts[0].shape, 1)
    turned = [pltpu.roll(p, LANES - 1, 1) for p in parts]
    turned.append(jnp.zeros_like(parts[0]))
    return [jnp.where(lane == LANES - 1, turned[i + 1], turned[i]) for i in range(len(parts))]


def z_down(parts):
    lane = lax.broadcasted_iota(jnp.int32, parts[0].shape, 1)
    turned = [jnp.zeros_like(parts[0])] + [pltpu.roll(p, 1, 1) for p in parts]
    return [jnp.where(lane == 0, turned[i], turned[i + 1]) for i in range(len(parts))]


def fine_kernel(
    rhs, visc, react, ids, x_low, x_high, y_low, y_high, c_low, c_high,
    vel_out, sums_out,
    visc_x, react_x, rhs_x, inv_x, wx, wy, wz, vel_a, vel_b, diag_s, terms,
):
    nx, ny, nz = visc.shape
    nc = nz // LANES

    def put(kind, c, x, rows, value):
        for i, part in enumerate(chunks_of(value)):
            if kind == "rhs":
                rhs_x[c, x, i, rows] = part
            elif kind == "visc":
                visc_x[x, i, rows] = part
            else:
                react_x[x, i, rows] = part

    own = pl.ds(Y0, ny)

    def fill(x, carry):
        for c in range(COMP):
            put("rhs", c, x + X0, own, rhs[c, x])
            at = pl.ds(c * WIDE, WIDE)
            put("rhs", c, x + X0, pl.ds(Y0 - WIDE, WIDE), y_low[x, at])
            put("rhs", c, x + X0, pl.ds(Y0 + ny, WIDE), y_high[x, at])
        put("visc", 0, x + X0, own, visc[x])
        at = pl.ds(VISC_AT, VWIDE)
        put("visc", 0, x + X0, pl.ds(Y0 - VWIDE, VWIDE), y_low[x, at])
        put("visc", 0, x + X0, pl.ds(Y0 + ny, VWIDE), y_high[x, at])
        put("react", 0, x + X0, own, react[x])
        at = pl.ds(REACT_AT, WIDE)
        put("react", 0, x + X0, pl.ds(Y0 - WIDE, WIDE), y_low[x, at])
        put("react", 0, x + X0, pl.ds(Y0 + ny, WIDE), y_high[x, at])
        return carry

    lax.fori_loop(0, nx, fill, 0)
    for side, source in enumerate((x_low, x_high)):
        for away in range(1, VWIDE + 1):
            x = X0 - away if side == 0 else X0 + nx - 1 + away
            put("visc", 0, x, own, source[halo_index(side, away, "visc", 0)])
            if away <= WIDE:
                for c in range(COMP):
                    put("rhs", c, x, own, source[halo_index(side, away, "rhs", c)])
                put("react", 0, x, own, source[halo_index(side, away, "react", 0)])
        for away, kind, c, at, count in corner_rows():
            x = X0 - away if side == 0 else X0 + nx - 1 + away
            put(kind, c, x, pl.ds(Y0 - count, count), c_low[side, pl.ds(at, count)])
            put(kind, c, x, pl.ds(Y0 + ny, count), c_high[side, pl.ds(at, count)])

    first, count = Y0 - WIDE, ny + 2 * WIDE
    mid = pl.ds(first, count)

    def prepare(x, carry):
        here = [visc_x[x, i, mid] for i in range(nc)]
        up = z_up(here)
        down = z_down(here)
        for i in range(nc):
            next_x = visc_x[x + 1, i, mid]
            next_y = visc_x[x, i, pl.ds(first + 1, count)]
            beside = next_x + visc_x[x - 1, i, mid]
            beside = beside + next_y + visc_x[x, i, pl.ds(first - 1, count)]
            beside = beside + up[i] + down[i]
            mass = react_x[x, i, mid]
            diag = mass + (3.0 * here[i] + 0.5 * beside)
            inv = jnp.where(mass > 0.0, 0.8 / diag, 0.0)
            diag_s[x, i, mid] = diag
            inv_x[x, i, mid] = inv
            wx[x, i, mid] = 0.5 * (here[i] + next_x)
            wy[x, i, mid] = 0.5 * (here[i] + next_y)
            wz[x, i, mid] = 0.5 * (here[i] + up[i])
            for c in range(COMP):
                vel_a[c, x, i, mid] = inv * rhs_x[c, x, i, mid]
        return carry

    lax.fori_loop(X0 - WIDE, X0 + nx + WIDE, prepare, 0)

    def besides(vel, c, x, first, count):
        rows = pl.ds(first, count)
        here = [vel[c, x, i, rows] for i in range(nc)]
        wz_here = [wz[x, i, rows] for i in range(nc)]
        up = z_up(here)
        down = z_down([wz_here[i] * here[i] for i in range(nc)])
        out = []
        for i in range(nc):
            total = wx[x, i, rows] * vel[c, x + 1, i, rows]
            total = total + wx[x - 1, i, rows] * vel[c, x - 1, i, rows]
            after, before = pl.ds(first + 1, count), pl.ds(first - 1, count)
            total = total + wy[x, i, rows] * vel[c, x, i, after]
            total = total + wy[x, i, before] * vel[c, x, i, before]
            out.append(total + wz_here[i] * up[i] + down[i])
        return here, out

    def sweep(source, target, reach):
        first, count = Y0 - reach, ny + 2 * reach
        rows = pl.ds(first, count)

        def step(x, carry):
            for c in range(COMP):
                here, beside = besides(source, c, x, first, count)
                for i in range(nc):
                    added = inv_x[x, i, rows] * (rhs_x[c, x, i, rows] + beside[i])
                    target[c, x, i, rows] = 0.2 * here[i] + added
            return carry

        lax.fori_loop(X0 - reach, X0 + nx + reach, step, 0)

    sweep(vel_a, vel_b, 2)
    sweep(vel_b, vel_a, 1)

    high = NAGG // LANES
    sub = lax.broadcasted_iota(jnp.int32, (2 * high, LANES), 0)
    in_high = sub % high
    is_first = sub < high
    label = lax.broadcasted_iota(jnp.int32, (LANES, LANES), 0)

    def gather(x, total):
        values = []
        for c in range(COMP):
            here, beside = besides(vel_a, c, x, Y0, ny)
            left = []
            for i in range(nc):
                vel_out[c, x - X0, :, i * LANES : (i + 1) * LANES] = here[i]
                left.append(rhs_x[c, x, i, own] - (diag_s[x, i, own] * here[i] - beside[i]))
            values.append(left)
        values.append([diag_s[x, i, own] for i in range(nc)])
        for t, value in enumerate(values):
            for i in range(nc):
                top = value[i].astype(jnp.bfloat16).astype(F32)
                terms[2 * t, i] = top
                terms[2 * t + 1, i] = value[i] - top
        for y in range(ny):
            left, right = [], []
            for i in range(nc):
                row = ids[x - X0, pl.ds(y, 1), i * LANES : (i + 1) * LANES]
                mask = (row >> 7) == in_high
                parts = []
                for t in range(COMP + 1):
                    top = terms[2 * t, i, pl.ds(y, 1)]
                    rest = terms[2 * t + 1, i, pl.ds(y, 1)]
                    parts.append(jnp.where(mask, jnp.where(is_first, top, rest), 0.0))
                left.append(jnp.concatenate(parts, axis=0).astype(jnp.bfloat16))
                hot = jnp.where((row & (LANES - 1)) == label, 1.0, 0.0)
                right.append(hot.astype(jnp.bfloat16))
            total = total + lax.dot_general(
                jnp.concatenate(left, axis=1),
                jnp.concatenate(right, axis=1),
                (((1,), (1,)), ((), ())),
                preferred_element_type=F32,
            )
        return total

    width = 2 * (COMP + 1) * high
    total = lax.fori_loop(X0, X0 + nx, gather, jnp.zeros((width, LANES), F32))
    for t in range(COMP + 1):
        at = 2 * high * t
        sums_out[pl.ds(high * t, high)] = total[at : at + high] + total[at + high : at + 2 * high]


def swapped(value, bit):
    row = lax.broadcasted_iota(jnp.int32, value.shape, 0)
    after = pltpu.roll(value, GROUP - bit, 0)
    before = pltpu.roll(value, bit, 0)
    return jnp.where((row & bit) == 0, after, before)


def coarse_kernel(place, arrived, out, levels):
    peers, rows, _ = arrived.shape
    flat = arrived.reshape(peers * rows, LANES)
    owner = flat[pl.ds(rows - 8, peers, stride=rows)]
    lane = lax.broadcasted_iota(jnp.int32, owner.shape, 1)
    base = place[0] - place[0] % GROUP
    chosen = jnp.where(owner == (base + lane).astype(F32), 1.0, 0.0)
    high = NAGG // LANES
    blocks = []
    for r in range((COMP + 1) * high):
        blocks.append(flat[pl.ds(r, peers, stride=rows)])
    gathered = jnp.concatenate(blocks, axis=1)
    owned = lax.dot_general(
        chosen, gathered, (((0,), (0,)), ((), ())),
        precision=lax.Precision.HIGHEST, preferred_element_type=F32,
    )[:GROUP]
    resid = [owned[:, c * NAGG : (c + 1) * NAGG] for c in range(COMP)]
    diag = 1.0 + owned[:, COMP * NAGG :]
    at = lax.broadcasted_iota(jnp.int32, diag.shape, 1)
    for level in range(MERGES + 1):
        coupling = 0.2 * jnp.minimum(diag, pltpu.roll(diag, NAGG - 1, 1))
        coupling = jnp.where(at == NAGG - 1, 0.0, coupling)

        def apply(vector):
            upper = coupling * pltpu.roll(vector, NAGG - 1, 1)
            lower = pltpu.roll(coupling * vector, 1, 1)
            return diag * vector - (upper + lower)

        left = []
        for c in range(COMP):
            correction = 0.8 * resid[c] / diag
            correction = correction + 0.8 * (resid[c] - apply(correction)) / diag
            levels[level, c] = correction
            out[level, pl.ds(c, 1)] = levels[level, c, pl.ds(place[0] % GROUP, 1)]
            if level < MERGES:
                rest = resid[c] - apply(correction)
                left.append(rest + swapped(rest, 2**level))
        if level < MERGES:
            resid = left
            diag = diag + swapped(diag, 2**level)


def shift(axis, value, by):
    count = lax.axis_size(axis)
    pairs = [(i, i + by) for i in range(count) if 0 <= i + by < count]
    return lax.ppermute(value, axis, pairs)


def shards(right_side, viscosity, reaction, agg_ids, owner_map):
    nx, ny, nz = viscosity.shape
    nc = nz // LANES
    x_message = jax.ShapeDtypeStruct((ROWS, ny, nz), F32)
    y_message = jax.ShapeDtypeStruct((nx, ROWS, nz), F32)
    to_x_low, to_x_high, to_y_low, to_y_high = pl.pallas_call(
        pack_faces,
        out_shape=(x_message, x_message, y_message, y_message),
        compiler_params=pltpu.CompilerParams(vmem_limit_bytes=BIG),
        name="pack_faces",
    )(right_side, viscosity, reaction)
    x_low = shift("gx", to_x_high, 1)
    x_high = shift("gx", to_x_low, -1)
    y_low = shift("gy", to_y_high, 1)
    y_high = shift("gy", to_y_low, -1)
    corner = jax.ShapeDtypeStruct((2, 24, nz), F32)
    to_c_low, to_c_high = pl.pallas_call(
        pack_corners,
        out_shape=(corner, corner),
        compiler_params=pltpu.CompilerParams(vmem_limit_bytes=BIG),
        name="pack_corners",
    )(x_low, x_high)
    c_low = shift("gy", to_c_high, 1)
    c_high = shift("gy", to_c_low, -1)

    wide = (nx + 2 * X0, nc, ny + 2 * Y0, LANES)
    high = NAGG // LANES
    velocity, sums = pl.pallas_call(
        fine_kernel,
        out_shape=(
            jax.ShapeDtypeStruct(right_side.shape, F32),
            jax.ShapeDtypeStruct(((COMP + 1) * high, LANES), F32),
        ),
        scratch_shapes=[
            pltpu.VMEM(wide, F32),
            pltpu.VMEM(wide, F32),
            pltpu.VMEM((COMP,) + wide, F32),
            pltpu.VMEM(wide, F32),
            pltpu.VMEM(wide, F32),
            pltpu.VMEM(wide, F32),
            pltpu.VMEM(wide, F32),
            pltpu.VMEM((COMP,) + wide, F32),
            pltpu.VMEM((COMP,) + wide, F32),
            pltpu.VMEM(wide, F32),
            pltpu.VMEM((2 * (COMP + 1), nc, ny, LANES), F32),
        ],
        compiler_params=pltpu.CompilerParams(vmem_limit_bytes=BIG),
        name="fine",
    )(right_side, viscosity, reaction, agg_ids, x_low, x_high, y_low, y_high, c_low, c_high)

    peers = lax.axis_size("gx")
    owner = jnp.broadcast_to(owner_map.astype(F32).reshape(1, 1), (8, LANES))
    packet = jnp.concatenate([sums, owner], axis=0)
    arrived = lax.all_to_all(
        jnp.broadcast_to(packet[None], (peers,) + packet.shape), "gx", 0, 0, tiled=True
    )
    place = lax.axis_index("gx").astype(jnp.int32).reshape(1)
    corrections = pl.pallas_call(
        coarse_kernel,
        out_shape=jax.ShapeDtypeStruct((MERGES + 1, COMP, NAGG), F32),
        in_specs=[
            pl.BlockSpec(memory_space=pltpu.SMEM),
            pl.BlockSpec(memory_space=pltpu.VMEM),
        ],
        scratch_shapes=[pltpu.VMEM((MERGES + 1, COMP, GROUP, NAGG), F32)],
        compiler_params=pltpu.CompilerParams(vmem_limit_bytes=BIG),
        name="coarse",
    )(place, arrived)
    return (velocity, corrections[None, None])


def solution(mesh):
    return jax.shard_map(
        shards,
        mesh=mesh,
        in_specs=(
            P(None, "gx", "gy", None),
            P("gx", "gy", None),
            P("gx", "gy", None),
            P("gx", "gy", None),
            P("gx", "gy"),
        ),
        out_specs=(P(None, "gx", "gy", None), P("gx", "gy", None, None, None)),
        check_vma=False,
    )
```

```python
import jax
import jax.numpy as jnp
from jax import lax
from jax.experimental import pallas as pl
from jax.experimental.pallas import tpu as pltpu
from jax.sharding import PartitionSpec as P

COMP = 3
NAGG = 512
MERGES = 3
GROUP = 2**MERGES
LANES = 128
WIDE = 3
VWIDE = WIDE + 1
VISC_AT = COMP * WIDE
REACT_AT = VISC_AT + VWIDE
ROWS = REACT_AT + WIDE
X0 = 4
Y0 = 8
F32 = jnp.float32
HIGH = 8
LOW = NAGG // HIGH
SUM_ROWS = (COMP + 1) * NAGG // LANES
BIG = 36 * 2**20
SMALL = 8 * 2**20


def pack_faces(rhs, visc, react, x_low, x_high, y_low, y_high):
    nx, ny, _ = visc.shape
    for c in range(COMP):
        for k in range(WIDE):
            x_low[c * WIDE + k] = rhs[c, k]
            x_high[c * WIDE + k] = rhs[c, nx - WIDE + k]
    for k in range(VWIDE):
        x_low[VISC_AT + k] = visc[k]
        x_high[VISC_AT + k] = visc[nx - VWIDE + k]
    for k in range(WIDE):
        x_low[REACT_AT + k] = react[k]
        x_high[REACT_AT + k] = react[nx - WIDE + k]
    for x in range(nx):
        for c in range(COMP):
            rows = pl.ds(c * WIDE, WIDE)
            y_low[x, rows] = rhs[c, x, pl.ds(0, WIDE)]
            y_high[x, rows] = rhs[c, x, pl.ds(ny - WIDE, WIDE)]
        rows = pl.ds(VISC_AT, VWIDE)
        y_low[x, rows] = visc[x, pl.ds(0, VWIDE)]
        y_high[x, rows] = visc[x, pl.ds(ny - VWIDE, VWIDE)]
        rows = pl.ds(REACT_AT, WIDE)
        y_low[x, rows] = react[x, pl.ds(0, WIDE)]
        y_high[x, rows] = react[x, pl.ds(ny - WIDE, WIDE)]


def corner_rows():
    table = []
    for away, at in ((1, 0), (2, 16), (3, 22)):
        left = WIDE - away
        if left:
            for c in range(COMP):
                table.append((away, "rhs", c, at, left))
                at += left
        table.append((away, "visc", 0, at, left + 1))
        at += left + 1
        if left:
            table.append((away, "react", 0, at, left))
    return table


def halo_index(side, away, kind, c):
    width = VWIDE if kind == "visc" else WIDE
    place = width - away if side == 0 else away - 1
    return {"rhs": c * WIDE, "visc": VISC_AT, "react": REACT_AT}[kind] + place


def pack_corners(from_low, from_high, y_low, y_high):
    ny = from_low.shape[1]
    for side, source in enumerate((from_low, from_high)):
        for away, kind, c, at, count in corner_rows():
            index = halo_index(side, away, kind, c)
            y_low[side, pl.ds(at, count)] = source[index, pl.ds(0, count)]
            y_high[side, pl.ds(at, count)] = source[index, pl.ds(ny - count, count)]


def chunks_of(value):
    return [value[..., c * LANES : (c + 1) * LANES] for c in range(value.shape[-1] // LANES)]


def z_up(parts):
    lane = lax.broadcasted_iota(jnp.int32, parts[0].shape, 1)
    turned = [pltpu.roll(p, LANES - 1, 1) for p in parts]
    turned.append(jnp.zeros_like(parts[0]))
    return [jnp.where(lane == LANES - 1, turned[i + 1], turned[i]) for i in range(len(parts))]


def z_down(parts):
    lane = lax.broadcasted_iota(jnp.int32, parts[0].shape, 1)
    turned = [jnp.zeros_like(parts[0])] + [pltpu.roll(p, 1, 1) for p in parts]
    return [jnp.where(lane == 0, turned[i], turned[i + 1]) for i in range(len(parts))]


def fine_kernel(
    owner, rhs, visc, react, ids, x_low, x_high, y_low, y_high, c_low, c_high,
    vel_out, packets,
    visc_x, react_x, rhs_x, inv_x, wx, wy, wz, vel_a, vel_b, diag_s, terms, low_s, high_s, sums,
):
    nx, ny, nz = visc.shape
    nc = nz // LANES

    def put(kind, c, x, rows, value):
        for i, part in enumerate(chunks_of(value)):
            if kind == "rhs":
                rhs_x[c, x, i, rows] = part
            elif kind == "visc":
                visc_x[x, i, rows] = part
            else:
                react_x[x, i, rows] = part

    own = pl.ds(Y0, ny)

    def fill(x, carry):
        for c in range(COMP):
            put("rhs", c, x + X0, own, rhs[c, x])
            at = pl.ds(c * WIDE, WIDE)
            put("rhs", c, x + X0, pl.ds(Y0 - WIDE, WIDE), y_low[x, at])
            put("rhs", c, x + X0, pl.ds(Y0 + ny, WIDE), y_high[x, at])
        put("visc", 0, x + X0, own, visc[x])
        at = pl.ds(VISC_AT, VWIDE)
        put("visc", 0, x + X0, pl.ds(Y0 - VWIDE, VWIDE), y_low[x, at])
        put("visc", 0, x + X0, pl.ds(Y0 + ny, VWIDE), y_high[x, at])
        put("react", 0, x + X0, own, react[x])
        at = pl.ds(REACT_AT, WIDE)
        put("react", 0, x + X0, pl.ds(Y0 - WIDE, WIDE), y_low[x, at])
        put("react", 0, x + X0, pl.ds(Y0 + ny, WIDE), y_high[x, at])
        return carry

    lax.fori_loop(0, nx, fill, 0)
    for side, source in enumerate((x_low, x_high)):
        for away in range(1, VWIDE + 1):
            x = X0 - away if side == 0 else X0 + nx - 1 + away
            put("visc", 0, x, own, source[halo_index(side, away, "visc", 0)])
            if away <= WIDE:
                for c in range(COMP):
                    put("rhs", c, x, own, source[halo_index(side, away, "rhs", c)])
                put("react", 0, x, own, source[halo_index(side, away, "react", 0)])
        for away, kind, c, at, count in corner_rows():
            x = X0 - away if side == 0 else X0 + nx - 1 + away
            put(kind, c, x, pl.ds(Y0 - count, count), c_low[side, pl.ds(at, count)])
            put(kind, c, x, pl.ds(Y0 + ny, count), c_high[side, pl.ds(at, count)])

    first, count = Y0 - WIDE, ny + 2 * WIDE
    mid = pl.ds(first, count)

    def prepare(x, carry):
        here = [visc_x[x, i, mid] for i in range(nc)]
        up = z_up(here)
        down = z_down(here)
        for i in range(nc):
            next_x = visc_x[x + 1, i, mid]
            next_y = visc_x[x, i, pl.ds(first + 1, count)]
            beside = next_x + visc_x[x - 1, i, mid]
            beside = beside + next_y + visc_x[x, i, pl.ds(first - 1, count)]
            beside = beside + up[i] + down[i]
            mass = react_x[x, i, mid]
            diag = mass + (3.0 * here[i] + 0.5 * beside)
            inv = jnp.where(mass > 0.0, 0.8 / diag, 0.0)
            diag_s[x, i, mid] = diag
            inv_x[x, i, mid] = inv
            wx[x, i, mid] = 0.5 * (here[i] + next_x)
            wy[x, i, mid] = 0.5 * (here[i] + next_y)
            wz[x, i, mid] = 0.5 * (here[i] + up[i])
            for c in range(COMP):
                vel_a[c, x, i, mid] = inv * rhs_x[c, x, i, mid]
        return carry

    lax.fori_loop(X0 - WIDE, X0 + nx + WIDE, prepare, 0)

    def besides(vel, c, x, first, count):
        rows = pl.ds(first, count)
        here = [vel[c, x, i, rows] for i in range(nc)]
        wz_here = [wz[x, i, rows] for i in range(nc)]
        up = z_up(here)
        down = z_down([wz_here[i] * here[i] for i in range(nc)])
        out = []
        for i in range(nc):
            total = wx[x, i, rows] * vel[c, x + 1, i, rows]
            total = total + wx[x - 1, i, rows] * vel[c, x - 1, i, rows]
            after, before = pl.ds(first + 1, count), pl.ds(first - 1, count)
            total = total + wy[x, i, rows] * vel[c, x, i, after]
            total = total + wy[x, i, before] * vel[c, x, i, before]
            out.append(total + wz_here[i] * up[i] + down[i])
        return here, out

    def sweep(source, target, reach):
        first, count = Y0 - reach, ny + 2 * reach
        rows = pl.ds(first, count)

        def step(x, carry):
            for c in range(COMP):
                here, beside = besides(source, c, x, first, count)
                for i in range(nc):
                    added = inv_x[x, i, rows] * (rhs_x[c, x, i, rows] + beside[i])
                    target[c, x, i, rows] = 0.2 * here[i] + added
            return carry

        lax.fori_loop(X0 - reach, X0 + nx + reach, step, 0)

    sweep(vel_a, vel_b, 2)
    sweep(vel_b, vel_a, 1)

    in_high = lax.broadcasted_iota(jnp.int32, (HIGH, LANES), 0)
    label = lax.broadcasted_iota(jnp.int32, (LOW, LANES), 0).astype(F32)
    label = label.astype(jnp.bfloat16).reshape(LOW // 16, 16, LANES)
    ones, zeros = jnp.ones_like(label), jnp.zeros_like(label)

    def gather(x, total):
        values = []
        for c in range(COMP):
            here, beside = besides(vel_a, c, x, Y0, ny)
            left = []
            for i in range(nc):
                vel_out[c, x - X0, :, i * LANES : (i + 1) * LANES] = here[i]
                left.append(rhs_x[c, x, i, own] - (diag_s[x, i, own] * here[i] - beside[i]))
            values.append(left)
        values.append([diag_s[x, i, own] for i in range(nc)])
        for t, value in enumerate(values):
            for i in range(nc):
                top = value[i].astype(jnp.bfloat16).astype(F32)
                terms[2 * t, i] = top
                terms[2 * t + 1, i] = value[i] - top
        for i in range(nc):
            ident = ids[x - X0, :, i * LANES : (i + 1) * LANES]
            low_s[i] = (ident % LOW).astype(F32)
            high_s[i] = ident // LOW
        for y in range(ny):
            left, right = [], []
            row = pl.ds(y, 1)
            for i in range(nc):
                mask = high_s[i, row] == in_high
                parts = [jnp.where(mask, terms[t, i, row], 0.0) for t in range(2 * (COMP + 1))]
                left.append(jnp.concatenate(parts, axis=0).astype(jnp.bfloat16))
                low = jnp.broadcast_to(low_s[i, row], (16, LANES)).astype(jnp.bfloat16)
                hot = jnp.where(low[None] == label, ones, zeros)
                right.append(hot.reshape(LOW, LANES))
            total = total + lax.dot_general(
                jnp.concatenate(left, axis=1),
                jnp.concatenate(right, axis=1),
                (((1,), (1,)), ((), ())),
                preferred_element_type=F32,
            )
        return total

    width = 2 * (COMP + 1) * HIGH
    total = lax.fori_loop(X0, X0 + nx, gather, jnp.zeros((width, LOW), F32))
    for t in range(COMP + 1):
        at = 2 * HIGH * t
        both = total[at : at + HIGH] + total[at + HIGH : at + 2 * HIGH]
        sums[pl.ds(HIGH * t, HIGH), pl.ds(0, LOW)] = both
    half = SUM_ROWS
    even = sums[pl.ds(0, half, stride=2)]
    odd = sums[pl.ds(1, half, stride=2)]
    lane = lax.broadcasted_iota(jnp.int32, even.shape, 1)
    packet = jnp.where(lane < LOW, even, pltpu.roll(odd, LOW, 1))
    mine = jnp.full((8, LANES), owner[0, 0], jnp.int32).astype(F32)
    for peer in range(packets.shape[0]):
        packets[peer, pl.ds(0, SUM_ROWS)] = packet
        packets[peer, pl.ds(SUM_ROWS, 8)] = mine


def swapped(value, bit):
    row = lax.broadcasted_iota(jnp.int32, value.shape, 0)
    after = pltpu.roll(value, GROUP - bit, 0)
    before = pltpu.roll(value, bit, 0)
    return jnp.where((row & bit) == 0, after, before)


def coarse_kernel(place, arrived, out, levels):
    peers, rows, _ = arrived.shape
    flat = arrived.reshape(peers * rows, LANES)
    owner = flat[pl.ds(rows - 8, peers, stride=rows)]
    lane = lax.broadcasted_iota(jnp.int32, owner.shape, 1)
    base = place[0] - place[0] % GROUP
    chosen = jnp.where(owner == (base + lane).astype(F32), 1.0, 0.0)
    blocks = []
    for r in range(SUM_ROWS):
        blocks.append(flat[pl.ds(r, peers, stride=rows)])
    gathered = jnp.concatenate(blocks, axis=1)
    owned = lax.dot_general(
        chosen, gathered, (((0,), (0,)), ((), ())),
        precision=lax.Precision.HIGHEST, preferred_element_type=F32,
    )[:GROUP]
    resid = [owned[:, c * NAGG : (c + 1) * NAGG] for c in range(COMP)]
    diag = 1.0 + owned[:, COMP * NAGG :]
    at = lax.broadcasted_iota(jnp.int32, diag.shape, 1)
    for level in range(MERGES + 1):
        coupling = 0.2 * jnp.minimum(diag, pltpu.roll(diag, NAGG - 1, 1))
        coupling = jnp.where(at == NAGG - 1, 0.0, coupling)

        def apply(vector):
            upper = coupling * pltpu.roll(vector, NAGG - 1, 1)
            lower = pltpu.roll(coupling * vector, 1, 1)
            return diag * vector - (upper + lower)

        left = []
        for c in range(COMP):
            correction = 0.8 * resid[c] / diag
            correction = correction + 0.8 * (resid[c] - apply(correction)) / diag
            levels[level, c] = correction
            out[c, pl.ds(level, 1)] = levels[level, c, pl.ds(place[0] % GROUP, 1)]
            if level < MERGES:
                rest = resid[c] - apply(correction)
                left.append(rest + swapped(rest, 2**level))
        if level < MERGES:
            resid = left
            diag = diag + swapped(diag, 2**level)


def shift(axis, value, by):
    count = lax.axis_size(axis)
    pairs = [(i, i + by) for i in range(count) if 0 <= i + by < count]
    return lax.ppermute(value, axis, pairs)


def shards(right_side, viscosity, reaction, agg_ids, owner_map):
    nx, ny, nz = viscosity.shape
    nc = nz // LANES
    x_message = jax.ShapeDtypeStruct((ROWS, ny, nz), F32)
    y_message = jax.ShapeDtypeStruct((nx, ROWS, nz), F32)
    to_x_low, to_x_high, to_y_low, to_y_high = pl.pallas_call(
        pack_faces,
        out_shape=(x_message, x_message, y_message, y_message),
        compiler_params=pltpu.CompilerParams(vmem_limit_bytes=SMALL),
        name="pack_faces",
    )(right_side, viscosity, reaction)
    x_low = shift("gx", to_x_high, 1)
    x_high = shift("gx", to_x_low, -1)
    y_low = shift("gy", to_y_high, 1)
    y_high = shift("gy", to_y_low, -1)
    corner = jax.ShapeDtypeStruct((2, 24, nz), F32)
    to_c_low, to_c_high = pl.pallas_call(
        pack_corners,
        out_shape=(corner, corner),
        compiler_params=pltpu.CompilerParams(vmem_limit_bytes=SMALL),
        name="pack_corners",
    )(x_low, x_high)
    c_low = shift("gy", to_c_high, 1)
    c_high = shift("gy", to_c_low, -1)

    wide = (nx + 2 * X0, nc, ny + 2 * Y0, LANES)
    peers = lax.axis_size("gx")
    velocity, packets = pl.pallas_call(
        fine_kernel,
        out_shape=(
            jax.ShapeDtypeStruct(right_side.shape, F32),
            jax.ShapeDtypeStruct((peers, SUM_ROWS + 8, LANES), F32),
        ),
        in_specs=[pl.BlockSpec(memory_space=pltpu.SMEM)]
        + [pl.BlockSpec(memory_space=pltpu.VMEM)] * 10,
        scratch_shapes=[
            pltpu.VMEM(wide, F32),
            pltpu.VMEM(wide, F32),
            pltpu.VMEM((COMP,) + wide, F32),
            pltpu.VMEM(wide, F32),
            pltpu.VMEM(wide, F32),
            pltpu.VMEM(wide, F32),
            pltpu.VMEM(wide, F32),
            pltpu.VMEM((COMP,) + wide, F32),
            pltpu.VMEM((COMP,) + wide, F32),
            pltpu.VMEM(wide, F32),
            pltpu.VMEM((2 * (COMP + 1), nc, ny, LANES), F32),
            pltpu.VMEM((nc, ny, LANES), F32),
            pltpu.VMEM((nc, ny, LANES), jnp.int32),
            pltpu.VMEM((2 * SUM_ROWS, LANES), F32),
        ],
        compiler_params=pltpu.CompilerParams(vmem_limit_bytes=BIG),
        name="fine",
    )(owner_map, right_side, viscosity, reaction, agg_ids, x_low, x_high, y_low, y_high, c_low, c_high)
    arrived = lax.all_to_all(packets, "gx", 0, 0, tiled=True)
    place = lax.axis_index("gx").astype(jnp.int32).reshape(1)
    corrections = pl.pallas_call(
        coarse_kernel,
        out_shape=jax.ShapeDtypeStruct((COMP, MERGES + 1, NAGG), F32),
        in_specs=[
            pl.BlockSpec(memory_space=pltpu.SMEM),
            pl.BlockSpec(memory_space=pltpu.VMEM),
        ],
        scratch_shapes=[pltpu.VMEM((MERGES + 1, COMP, GROUP, NAGG), F32)],
        compiler_params=pltpu.CompilerParams(vmem_limit_bytes=SMALL),
        name="coarse",
    )(place, arrived)
    return (velocity, corrections.transpose(1, 0, 2)[None, None])


def solution(mesh):
    return jax.shard_map(
        shards,
        mesh=mesh,
        in_specs=(
            P(None, "gx", "gy", None),
            P("gx", "gy", None),
            P("gx", "gy", None),
            P("gx", "gy", None),
            P("gx", "gy"),
        ),
        out_specs=(P(None, "gx", "gy", None), P("gx", "gy", None, None, None)),
        check_vma=False,
    )
```

```python
import jax
import jax.numpy as jnp
from jax import lax
from jax.experimental import pallas as pl
from jax.experimental.pallas import tpu as pltpu
from jax.sharding import PartitionSpec as P

COMP = 3
NAGG = 512
MERGES = 3
GROUP = 2**MERGES
LANES = 128
WIDE = 3
VWIDE = WIDE + 1
VISC_AT = COMP * WIDE
REACT_AT = VISC_AT + VWIDE
ROWS = REACT_AT + WIDE
X0 = VWIDE
Y0 = VWIDE
F32 = jnp.float32
HIGH = 8
LOW = NAGG // HIGH
SUM_ROWS = (COMP + 1) * NAGG // LANES
BIG = 32 * 2**20
SMALL = 8 * 2**20


def corner_rows():
    table = []
    for away, at in ((1, 0), (2, 16), (3, 22)):
        left = WIDE - away
        if left:
            for c in range(COMP):
                table.append((away, "rhs", c, at, left))
                at += left
        table.append((away, "visc", 0, at, left + 1))
        at += left + 1
        if left:
            table.append((away, "react", 0, at, left))
    return table


def pack_y(rhs, visc, react, y_low, y_high):
    nx, ny, _ = visc.shape
    for x in range(nx):
        for c in range(COMP):
            rows = pl.ds(c * WIDE, WIDE)
            y_low[x, rows] = rhs[c, x, pl.ds(0, WIDE)]
            y_high[x, rows] = rhs[c, x, pl.ds(ny - WIDE, WIDE)]
        rows = pl.ds(VISC_AT, VWIDE)
        y_low[x, rows] = visc[x, pl.ds(0, VWIDE)]
        y_high[x, rows] = visc[x, pl.ds(ny - VWIDE, VWIDE)]
        rows = pl.ds(REACT_AT, WIDE)
        y_low[x, rows] = react[x, pl.ds(0, WIDE)]
        y_high[x, rows] = react[x, pl.ds(ny - WIDE, WIDE)]


def pack_corners(place, near, far, c_low, c_high):
    ny = near.shape[1]
    even = place[0] % 2 == 0
    for side, (source, at_high) in enumerate(((near, even), (far, jnp.logical_not(even)))):
        for away, kind, c, at, count in corner_rows():
            width = VWIDE if kind == "visc" else WIDE
            first = {"rhs": c * WIDE, "visc": VISC_AT, "react": REACT_AT}[kind]
            index = first + jnp.where(at_high, away - 1, width - away)
            rows = pl.ds(at, count)
            c_low[side, rows] = source[index, pl.ds(0, count)]
            c_high[side, rows] = source[index, pl.ds(ny - count, count)]


def chunks_of(value):
    return [value[..., c * LANES : (c + 1) * LANES] for c in range(value.shape[-1] // LANES)]


def z_up(parts):
    lane = lax.broadcasted_iota(jnp.int32, parts[0].shape, 1)
    turned = [pltpu.roll(p, LANES - 1, 1) for p in parts]
    turned.append(jnp.zeros_like(parts[0]))
    return [jnp.where(lane == LANES - 1, turned[i + 1], turned[i]) for i in range(len(parts))]


def z_down(parts):
    lane = lax.broadcasted_iota(jnp.int32, parts[0].shape, 1)
    turned = [jnp.zeros_like(parts[0])] + [pltpu.roll(p, 1, 1) for p in parts]
    return [jnp.where(lane == 0, turned[i], turned[i + 1]) for i in range(len(parts))]


def fine_kernel(
    place, owner, rhs, visc, react, ids, near, far, y_low, y_high, c_low, c_high,
    vel_out, packets,
    half_x, react_x, rhs_x, inv_x, vel_a, vel_b, diag_s, terms, low_s, high_s, sums,
):
    nx, ny, nz = visc.shape
    nc = nz // LANES

    def put(kind, c, x, rows, value):
        for i, part in enumerate(chunks_of(value)):
            if kind == "rhs":
                rhs_x[c, x, i, rows] = part
            elif kind == "visc":
                half_x[x, i, rows] = 0.5 * part
            else:
                react_x[x, i, rows] = part

    own = pl.ds(Y0, ny)

    def fill(x, carry):
        for c in range(COMP):
            put("rhs", c, x + X0, own, rhs[c, x])
            at = pl.ds(c * WIDE, WIDE)
            put("rhs", c, x + X0, pl.ds(Y0 - WIDE, WIDE), y_low[x, at])
            put("rhs", c, x + X0, pl.ds(Y0 + ny, WIDE), y_high[x, at])
        put("visc", 0, x + X0, own, visc[x])
        at = pl.ds(VISC_AT, VWIDE)
        put("visc", 0, x + X0, pl.ds(Y0 - VWIDE, VWIDE), y_low[x, at])
        put("visc", 0, x + X0, pl.ds(Y0 + ny, VWIDE), y_high[x, at])
        put("react", 0, x + X0, own, react[x])
        at = pl.ds(REACT_AT, WIDE)
        put("react", 0, x + X0, pl.ds(Y0 - WIDE, WIDE), y_low[x, at])
        put("react", 0, x + X0, pl.ds(Y0 + ny, WIDE), y_high[x, at])
        return carry

    lax.fori_loop(0, nx, fill, 0)
    even = place[0] % 2 == 0
    for source, at_high in ((near, even), (far, jnp.logical_not(even))):
        for away in range(1, VWIDE + 1):
            x = jnp.where(at_high, X0 + nx - 1 + away, X0 - away)
            place_v = jnp.where(at_high, away - 1, VWIDE - away)
            put("visc", 0, x, own, source[VISC_AT + place_v])
            if away <= WIDE:
                place_w = jnp.where(at_high, away - 1, WIDE - away)
                for c in range(COMP):
                    put("rhs", c, x, own, source[c * WIDE + place_w])
                put("react", 0, x, own, source[REACT_AT + place_w])
    for side, at_high in enumerate((even, jnp.logical_not(even))):
        for away, kind, c, at, count in corner_rows():
            before, after = pl.ds(Y0 - count, count), pl.ds(Y0 + ny, count)
            x = jnp.where(at_high, X0 + nx - 1 + away, X0 - away)
            put(kind, c, x, before, c_low[side, pl.ds(at, count)])
            put(kind, c, x, after, c_high[side, pl.ds(at, count)])

    def y_up(value):
        return pltpu.roll(value, value.shape[0] - 1, 0)

    def y_down(value):
        return pltpu.roll(value, 1, 0)

    def prepare(x, carry):
        here = [half_x[x, i] for i in range(nc)]
        up = z_up(here)
        down = z_down(here)
        for i in range(nc):
            beside = half_x[x + 1, i] + half_x[x - 1, i]
            beside = beside + y_up(here[i]) + y_down(here[i])
            beside = beside + up[i] + down[i]
            mass = react_x[x, i]
            diag = mass + (6.0 * here[i] + beside)
            inv = jnp.where(mass > 0.0, 0.8 / diag, 0.0)
            diag_s[x, i] = diag
            inv_x[x, i] = inv
            for c in range(COMP):
                vel_a[c, x, i] = inv * rhs_x[c, x, i]
        return carry

    lax.fori_loop(X0 - WIDE, X0 + nx + WIDE, prepare, 0, unroll=11)

    def stencil(vel, x, emit):
        shape = half_x.shape[2:]
        lane = lax.broadcasted_iota(jnp.int32, shape, 1)
        is_first, is_last = lane == 0, lane == LANES - 1
        none = jnp.zeros(shape, F32)
        half = [half_x[x, i] for i in range(nc)]
        half_up = [pltpu.roll(h, LANES - 1, 1) for h in half] + [none]
        here = [[vel[c, x, i] for i in range(nc)] for c in range(COMP)]
        turned = [[pltpu.roll(h, LANES - 1, 1) for h in part] + [none] for part in here]
        last = [none] * COMP
        for i in range(nc):
            w_x = half[i] + half_x[x + 1, i]
            w_x_before = half[i] + half_x[x - 1, i]
            w_y = half[i] + y_up(half[i])
            w_z = half[i] + jnp.where(is_last, half_up[i + 1], half_up[i])
            for c in range(COMP):
                up = jnp.where(is_last, turned[c][i + 1], turned[c][i])
                down = pltpu.roll(w_z * here[c][i], 1, 1)
                total = w_x * vel[c, x + 1, i] + w_x_before * vel[c, x - 1, i]
                total = total + w_y * y_up(here[c][i]) + y_down(w_y * here[c][i])
                total = total + w_z * up + jnp.where(is_first, last[c], down)
                last[c] = down
                emit(c, i, here[c][i], total)

    def sweep(source, target, reach, unroll):
        def step(x, carry):
            def emit(c, i, here, beside):
                added = inv_x[x, i] * (rhs_x[c, x, i] + beside)
                target[c, x, i] = 0.2 * here + added

            stencil(source, x, emit)
            return carry

        lax.fori_loop(X0 - reach, X0 + nx + reach, step, 0, unroll=unroll)

    sweep(vel_a, vel_b, 2, 10)
    sweep(vel_b, vel_a, 1, 9)

    in_high = lax.broadcasted_iota(jnp.int32, (HIGH, LANES), 0)
    label = lax.broadcasted_iota(jnp.int32, (LOW, LANES), 0).astype(F32)
    label = label.astype(jnp.bfloat16).reshape(LOW // 16, 16, LANES)
    ones, zeros = jnp.ones_like(label), jnp.zeros_like(label)

    def gather(x, total):
        def split(t, i, value):
            top = value.astype(jnp.bfloat16).astype(F32)
            terms[2 * t, i] = top
            terms[2 * t + 1, i] = value - top

        def emit(c, i, here, beside):
            vel_out[c, x - X0, :, i * LANES : (i + 1) * LANES] = here[Y0 : Y0 + ny]
            split(c, i, rhs_x[c, x, i] - (diag_s[x, i] * here - beside))

        stencil(vel_a, x, emit)
        for i in range(nc):
            split(COMP, i, diag_s[x, i])
        for i in range(nc):
            ident = ids[x - X0, :, i * LANES : (i + 1) * LANES]
            low_s[i] = (ident % LOW).astype(F32)
            high_s[i] = ident // LOW
        for y in range(ny):
            left, right = [], []
            row, at = pl.ds(y, 1), pl.ds(Y0 + y, 1)
            for i in range(nc):
                mask = high_s[i, row] == in_high
                parts = [jnp.where(mask, terms[t, i, at], 0.0) for t in range(2 * (COMP + 1))]
                left.append(jnp.concatenate(parts, axis=0).astype(jnp.bfloat16))
                low = jnp.broadcast_to(low_s[i, row], (16, LANES)).astype(jnp.bfloat16)
                hot = jnp.where(low[None] == label, ones, zeros)
                right.append(hot.reshape(LOW, LANES))
            total = total + lax.dot_general(
                jnp.concatenate(left, axis=1),
                jnp.concatenate(right, axis=1),
                (((1,), (1,)), ((), ())),
                preferred_element_type=F32,
            )
        return total

    width = 2 * (COMP + 1) * HIGH
    total = lax.fori_loop(X0, X0 + nx, gather, jnp.zeros((width, LOW), F32), unroll=4)
    for t in range(COMP + 1):
        at = 2 * HIGH * t
        both = total[at : at + HIGH] + total[at + HIGH : at + 2 * HIGH]
        sums[pl.ds(HIGH * t, HIGH), pl.ds(0, LOW)] = both
    half = SUM_ROWS
    even = sums[pl.ds(0, half, stride=2)]
    odd = sums[pl.ds(1, half, stride=2)]
    lane = lax.broadcasted_iota(jnp.int32, even.shape, 1)
    packet = jnp.where(lane < LOW, even, pltpu.roll(odd, LOW, 1))
    mine = jnp.full((8, LANES), owner[0, 0], jnp.int32).astype(F32)
    for peer in range(packets.shape[0]):
        packets[peer, pl.ds(0, SUM_ROWS)] = packet
        packets[peer, pl.ds(SUM_ROWS, 8)] = mine


def swapped(value, bit):
    row = lax.broadcasted_iota(jnp.int32, value.shape, 0)
    after = pltpu.roll(value, GROUP - bit, 0)
    before = pltpu.roll(value, bit, 0)
    return jnp.where((row & bit) == 0, after, before)


def coarse_kernel(place, arrived, out, levels):
    peers, rows, _ = arrived.shape
    flat = arrived.reshape(peers * rows, LANES)
    owner = flat[pl.ds(rows - 8, peers, stride=rows)]
    lane = lax.broadcasted_iota(jnp.int32, owner.shape, 1)
    base = place[0] - place[0] % GROUP
    chosen = jnp.where(owner == (base + lane).astype(F32), 1.0, 0.0)[:, :GROUP]
    blocks = []
    for r in range(SUM_ROWS):
        blocks.append(flat[pl.ds(r, peers, stride=rows)])
    gathered = jnp.concatenate(blocks, axis=1)
    owned = lax.dot_general(
        chosen, gathered, (((0,), (0,)), ((), ())),
        precision=lax.Precision.HIGHEST, preferred_element_type=F32,
    )
    resid = [owned[:, c * NAGG : (c + 1) * NAGG] for c in range(COMP)]
    diag = 1.0 + owned[:, COMP * NAGG :]
    at = lax.broadcasted_iota(jnp.int32, diag.shape, 1)
    for level in range(MERGES + 1):
        coupling = 0.2 * jnp.minimum(diag, pltpu.roll(diag, NAGG - 1, 1))
        coupling = jnp.where(at == NAGG - 1, 0.0, coupling)

        def apply(vector):
            upper = coupling * pltpu.roll(vector, NAGG - 1, 1)
            lower = pltpu.roll(coupling * vector, 1, 1)
            return diag * vector - (upper + lower)

        left = []
        for c in range(COMP):
            correction = 0.8 * resid[c] / diag
            correction = correction + 0.8 * (resid[c] - apply(correction)) / diag
            levels[level, c] = correction
            out[c, pl.ds(level, 1)] = levels[level, c, pl.ds(place[0] % GROUP, 1)]
            if level < MERGES:
                rest = resid[c] - apply(correction)
                left.append(rest + swapped(rest, 2**level))
        if level < MERGES:
            resid = left
            diag = diag + swapped(diag, 2**level)


def shift(axis, value, by):
    count = lax.axis_size(axis)
    pairs = [(i, i + by) for i in range(count) if 0 <= i + by < count]
    return lax.ppermute(value, axis, pairs)


def shards(right_side, viscosity, reaction, agg_ids, owner_map):
    nx, ny, nz = viscosity.shape
    nc = nz // LANES
    width = lax.axis_size("gx")
    place = lax.axis_index("gx").astype(jnp.int32).reshape(1)
    smem = pl.BlockSpec(memory_space=pltpu.SMEM)
    vmem = pl.BlockSpec(memory_space=pltpu.VMEM)
    small = pltpu.CompilerParams(vmem_limit_bytes=SMALL)

    def face(at_high):
        first = jnp.where(at_high, nx - WIDE, 0)
        first_v = jnp.where(at_high, nx - VWIDE, 0)
        return jnp.concatenate(
            [
                lax.dynamic_slice_in_dim(right_side, first, WIDE, axis=1).reshape(-1, ny, nz),
                lax.dynamic_slice_in_dim(viscosity, first_v, VWIDE, axis=0),
                lax.dynamic_slice_in_dim(reaction, first, WIDE, axis=0),
            ],
            axis=0,
        )

    even = place[0] % 2 == 0
    to_far, to_near = face(jnp.logical_not(even)), face(even)
    beyond = [(i, i - 1 if i % 2 == 0 else i + 1) for i in range(width)]
    beyond = [(i, k) for i, k in beyond if 0 <= k < width]
    far = lax.ppermute(to_far, "gx", beyond)
    near = lax.ppermute(to_near, "gx", [(i, i ^ 1) for i in range(width)])
    y_message = jax.ShapeDtypeStruct((nx, ROWS, nz), F32)
    to_y_low, to_y_high = pl.pallas_call(
        pack_y,
        out_shape=(y_message, y_message),
        compiler_params=small,
        name="pack_y",
    )(right_side, viscosity, reaction)
    y_low = shift("gy", to_y_high, 1)
    y_high = shift("gy", to_y_low, -1)
    corner = jax.ShapeDtypeStruct((2, 24, nz), F32)
    to_c_low, to_c_high = pl.pallas_call(
        pack_corners,
        out_shape=(corner, corner),
        in_specs=[smem, vmem, vmem],
        compiler_params=small,
        name="pack_corners",
    )(place, near, far)
    c_low = shift("gy", to_c_high, 1)
    c_high = shift("gy", to_c_low, -1)

    wide = (nx + 2 * X0, nc, ny + 2 * Y0, LANES)
    velocity, packets = pl.pallas_call(
        fine_kernel,
        out_shape=(
            jax.ShapeDtypeStruct(right_side.shape, F32),
            jax.ShapeDtypeStruct((width, SUM_ROWS + 8, LANES), F32),
        ),
        in_specs=[smem, smem] + [vmem] * 10,
        scratch_shapes=[
            pltpu.VMEM(wide, F32),
            pltpu.VMEM(wide, F32),
            pltpu.VMEM((COMP,) + wide, F32),
            pltpu.VMEM(wide, F32),
            pltpu.VMEM((COMP,) + wide, F32),
            pltpu.VMEM((COMP,) + wide, F32),
            pltpu.VMEM(wide, F32),
            pltpu.VMEM((2 * (COMP + 1),) + wide[1:], F32),
            pltpu.VMEM((nc, ny, LANES), F32),
            pltpu.VMEM((nc, ny, LANES), jnp.int32),
            pltpu.VMEM((2 * SUM_ROWS, LANES), F32),
        ],
        compiler_params=pltpu.CompilerParams(vmem_limit_bytes=BIG),
        name="fine",
    )(
        place, owner_map, right_side, viscosity, reaction, agg_ids,
        near, far, y_low, y_high, c_low, c_high,
    )
    arrived = lax.all_to_all(packets, "gx", 0, 0, tiled=True)
    corrections = pl.pallas_call(
        coarse_kernel,
        out_shape=jax.ShapeDtypeStruct((COMP, MERGES + 1, NAGG), F32),
        in_specs=[smem, vmem],
        scratch_shapes=[pltpu.VMEM((MERGES + 1, COMP, GROUP, NAGG), F32)],
        compiler_params=small,
        name="coarse",
    )(place, arrived)
    return (velocity, corrections.transpose(1, 0, 2)[None, None])


def solution(mesh):
    return jax.shard_map(
        shards,
        mesh=mesh,
        in_specs=(
            P(None, "gx", "gy", None),
            P("gx", "gy", None),
            P("gx", "gy", None),
            P("gx", "gy", None),
            P("gx", "gy"),
        ),
        out_specs=(P(None, "gx", "gy", None), P("gx", "gy", None, None, None)),
        check_vma=False,
    )
```

```python
import jax
import jax.numpy as jnp
from jax import lax
from jax.experimental import pallas as pl
from jax.experimental.pallas import tpu as pltpu
from jax.sharding import PartitionSpec as P

COMP = 3
NAGG = 512
MERGES = 3
GROUP = 2**MERGES
LANES = 128
WIDE = 3
VWIDE = WIDE + 1
VISC_AT = COMP * WIDE
REACT_AT = VISC_AT + VWIDE
ROWS = REACT_AT + WIDE
Y_VISC_AT = COMP * WIDE
Y_REACT_AT = Y_VISC_AT + WIDE
Y_ROWS = Y_REACT_AT + WIDE
CORNER = 18
X0 = VWIDE
Y0 = VWIDE
F32 = jnp.float32
HIGH = 8
LOW = NAGG // HIGH
SUM_ROWS = (COMP + 1) * NAGG // LANES
BIG = 32 * 2**20
SMALL = 8 * 2**20


def corner_rows():
    table = []
    for away, at in ((1, 0), (2, 11), (3, 17)):
        left = WIDE - away
        if left:
            for c in range(COMP):
                table.append((away, "rhs", c, at, left))
                at += left
        table.append((away, "visc", 0, at, left + 1))
        at += left + 1
        if left:
            table.append((away, "react", 0, at, left))
    return table


def pack_y(rhs, visc, react, y_low, y_high):
    nx, ny, _ = visc.shape
    for x in range(nx):
        at = x * Y_ROWS
        for c in range(COMP):
            rows = pl.ds(at + c * WIDE, WIDE)
            y_low[rows] = rhs[c, x, pl.ds(0, WIDE)]
            y_high[rows] = rhs[c, x, pl.ds(ny - WIDE, WIDE)]
        rows = pl.ds(at + Y_VISC_AT, WIDE)
        y_low[rows] = visc[x, pl.ds(0, WIDE)]
        y_high[rows] = visc[x, pl.ds(ny - WIDE, WIDE)]
        at = at + Y_REACT_AT
        y_low[pl.ds(at, WIDE - 1)] = react[x, pl.ds(0, WIDE - 1)]
        last = react[x, pl.ds(WIDE - 1, 1)] + 0.5 * visc[x, pl.ds(WIDE, 1)]
        y_low[pl.ds(at + WIDE - 1, 1)] = last
        last = react[x, pl.ds(ny - WIDE, 1)] + 0.5 * visc[x, pl.ds(ny - WIDE - 1, 1)]
        y_high[pl.ds(at, 1)] = last
        y_high[pl.ds(at + 1, WIDE - 1)] = react[x, pl.ds(ny - WIDE + 1, WIDE - 1)]


def pack_corners(place, near, far, c_low, c_high):
    ny = near.shape[1]
    even = place[0] % 2 == 0
    for side, (source, at_high) in enumerate(((near, even), (far, jnp.logical_not(even)))):
        for away, kind, c, at, count in corner_rows():
            width = VWIDE if kind == "visc" else WIDE
            first = {"rhs": c * WIDE, "visc": VISC_AT, "react": REACT_AT}[kind]
            index = first + jnp.where(at_high, away - 1, width - away)
            rows = pl.ds(side * CORNER + at, count)
            c_low[rows] = source[index, pl.ds(0, count)]
            c_high[rows] = source[index, pl.ds(ny - count, count)]


def chunks_of(value):
    return [value[..., c * LANES : (c + 1) * LANES] for c in range(value.shape[-1] // LANES)]


def z_up(parts):
    lane = lax.broadcasted_iota(jnp.int32, parts[0].shape, 1)
    turned = [pltpu.roll(p, LANES - 1, 1) for p in parts]
    turned.append(jnp.zeros_like(parts[0]))
    return [jnp.where(lane == LANES - 1, turned[i + 1], turned[i]) for i in range(len(parts))]


def z_down(parts):
    lane = lax.broadcasted_iota(jnp.int32, parts[0].shape, 1)
    turned = [jnp.zeros_like(parts[0])] + [pltpu.roll(p, 1, 1) for p in parts]
    return [jnp.where(lane == 0, turned[i], turned[i + 1]) for i in range(len(parts))]


def fine_kernel(
    place, owner, rhs, visc, react, ids, near, far, y_low, y_high, c_low, c_high,
    vel_out, packets,
    half_x, react_x, rhs_x, inv_x, vel_a, vel_b, diag_s, terms, low_s, high_s, sums, vel_s, sems,
):
    nx, ny, nz = visc.shape
    nc = nz // LANES

    def put(kind, c, x, rows, value):
        for i, part in enumerate(chunks_of(value)):
            if kind == "rhs":
                rhs_x[c, x, i, rows] = part
            elif kind == "visc":
                half_x[x, i, rows] = 0.5 * part
            else:
                react_x[x, i, rows] = part

    own = pl.ds(Y0, ny)

    before, after = pl.ds(Y0 - WIDE, WIDE), pl.ds(Y0 + ny, WIDE)
    nothing = jnp.zeros((1, nz), F32)
    for x in range(nx):
        at = x * Y_ROWS
        for c in range(COMP):
            put("rhs", c, x + X0, own, rhs[c, x])
            rows = pl.ds(at + c * WIDE, WIDE)
            put("rhs", c, x + X0, before, y_low[rows])
            put("rhs", c, x + X0, after, y_high[rows])
        put("visc", 0, x + X0, own, visc[x])
        rows = pl.ds(at + Y_VISC_AT, WIDE)
        put("visc", 0, x + X0, before, y_low[rows])
        put("visc", 0, x + X0, after, y_high[rows])
        put("visc", 0, x + X0, pl.ds(Y0 - VWIDE, 1), nothing)
        put("visc", 0, x + X0, pl.ds(Y0 + ny + WIDE, 1), nothing)
        put("react", 0, x + X0, own, react[x])
        rows = pl.ds(at + Y_REACT_AT, WIDE)
        put("react", 0, x + X0, before, y_low[rows])
        put("react", 0, x + X0, after, y_high[rows])
    even = place[0] % 2 == 0
    for source, at_high in ((near, even), (far, jnp.logical_not(even))):
        for away in range(1, VWIDE + 1):
            x = jnp.where(at_high, X0 + nx - 1 + away, X0 - away)
            place_v = jnp.where(at_high, away - 1, VWIDE - away)
            put("visc", 0, x, own, source[VISC_AT + place_v])
            if away <= WIDE:
                place_w = jnp.where(at_high, away - 1, WIDE - away)
                for c in range(COMP):
                    put("rhs", c, x, own, source[c * WIDE + place_w])
                put("react", 0, x, own, source[REACT_AT + place_w])
    for side, at_high in enumerate((even, jnp.logical_not(even))):
        for away, kind, c, at, count in corner_rows():
            before, after = pl.ds(Y0 - count, count), pl.ds(Y0 + ny, count)
            x = jnp.where(at_high, X0 + nx - 1 + away, X0 - away)
            rows = pl.ds(side * CORNER + at, count)
            put(kind, c, x, before, c_low[rows])
            put(kind, c, x, after, c_high[rows])

    def y_up(value):
        return pltpu.roll(value, value.shape[0] - 1, 0)

    def y_down(value):
        return pltpu.roll(value, 1, 0)

    def prepare(x, carry):
        here = [half_x[x, i] for i in range(nc)]
        up = z_up(here)
        down = z_down(here)
        for i in range(nc):
            beside = half_x[x + 1, i] + half_x[x - 1, i]
            beside = beside + y_up(here[i]) + y_down(here[i])
            beside = beside + up[i] + down[i]
            mass = react_x[x, i]
            diag = mass + (6.0 * here[i] + beside)
            inv = jnp.where(mass > 0.0, 0.8 / diag, 0.0)
            diag_s[x, i] = diag
            inv_x[x, i] = inv
            for c in range(COMP):
                vel_a[c, x, i] = inv * rhs_x[c, x, i]
        return carry

    lax.fori_loop(X0 - WIDE, X0 + nx + WIDE, prepare, 0, unroll=True)

    def stencil(vel, x, emit):
        shape = half_x.shape[2:]
        lane = lax.broadcasted_iota(jnp.int32, shape, 1)
        is_first, is_last = lane == 0, lane == LANES - 1
        none = jnp.zeros(shape, F32)
        half = [half_x[x, i] for i in range(nc)]
        half_up = [pltpu.roll(h, LANES - 1, 1) for h in half] + [none]
        here = [[vel[c, x, i] for i in range(nc)] for c in range(COMP)]
        turned = [[pltpu.roll(h, LANES - 1, 1) for h in part] + [none] for part in here]
        last = [none] * COMP
        for i in range(nc):
            w_x = half[i] + half_x[x + 1, i]
            w_x_before = half[i] + half_x[x - 1, i]
            w_y = half[i] + y_up(half[i])
            w_z = half[i] + jnp.where(is_last, half_up[i + 1], half_up[i])
            for c in range(COMP):
                up = jnp.where(is_last, turned[c][i + 1], turned[c][i])
                down = pltpu.roll(w_z * here[c][i], 1, 1)
                total = w_x * vel[c, x + 1, i] + w_x_before * vel[c, x - 1, i]
                total = total + w_y * y_up(here[c][i]) + y_down(w_y * here[c][i])
                total = total + w_z * up + jnp.where(is_first, last[c], down)
                last[c] = down
                emit(c, i, here[c][i], total)

    def sweep(source, target, reach):
        def step(x, carry):
            def emit(c, i, here, beside):
                added = inv_x[x, i] * (rhs_x[c, x, i] + beside)
                target[c, x, i] = 0.2 * here + added

            stencil(source, x, emit)
            return carry

        lax.fori_loop(X0 - reach, X0 + nx + reach, step, 0, unroll=True)

    sweep(vel_a, vel_b, 2)
    sweep(vel_b, vel_a, 1)

    in_high = lax.broadcasted_iota(jnp.int32, (HIGH, LANES), 0)
    label = lax.broadcasted_iota(jnp.int32, (LOW, LANES), 0).astype(F32)
    label = label.astype(jnp.bfloat16).reshape(LOW // 16, 16, LANES)
    ones, zeros = jnp.ones_like(label), jnp.zeros_like(label)

    def leave(x):
        return pltpu.make_async_copy(vel_s.at[:, x], vel_out.at[:, x], sems.at[x])

    def gather(x, total):
        def split(t, i, value):
            top = value.astype(jnp.bfloat16).astype(F32)
            terms[2 * t, i] = top
            terms[2 * t + 1, i] = value - top

        def emit(c, i, here, beside):
            vel_s[c, x - X0, :, i * LANES : (i + 1) * LANES] = here[Y0 : Y0 + ny]
            split(c, i, rhs_x[c, x, i] - (diag_s[x, i] * here - beside))

        stencil(vel_a, x, emit)
        leave(x - X0).start()
        for i in range(nc):
            split(COMP, i, diag_s[x, i])
        for i in range(nc):
            ident = ids[x - X0, :, i * LANES : (i + 1) * LANES]
            low_s[i] = (ident % LOW).astype(F32)
            high_s[i] = ident // LOW
        for y in range(ny):
            left, right = [], []
            row, at = pl.ds(y, 1), pl.ds(Y0 + y, 1)
            for i in range(nc):
                mask = high_s[i, row] == in_high
                parts = [jnp.where(mask, terms[t, i, at], 0.0) for t in range(2 * (COMP + 1))]
                left.append(jnp.concatenate(parts, axis=0).astype(jnp.bfloat16))
                low = jnp.broadcast_to(low_s[i, row], (16, LANES)).astype(jnp.bfloat16)
                hot = jnp.where(low[None] == label, ones, zeros)
                right.append(hot.reshape(LOW, LANES))
            total = total + lax.dot_general(
                jnp.concatenate(left, axis=1),
                jnp.concatenate(right, axis=1),
                (((1,), (1,)), ((), ())),
                preferred_element_type=F32,
            )
        return total

    width = 2 * (COMP + 1) * HIGH
    total = lax.fori_loop(X0, X0 + nx, gather, jnp.zeros((width, LOW), F32), unroll=4)
    for t in range(COMP + 1):
        at = 2 * HIGH * t
        both = total[at : at + HIGH] + total[at + HIGH : at + 2 * HIGH]
        sums[pl.ds(HIGH * t, HIGH), pl.ds(0, LOW)] = both
    half = SUM_ROWS
    even = sums[pl.ds(0, half, stride=2)]
    odd = sums[pl.ds(1, half, stride=2)]
    lane = lax.broadcasted_iota(jnp.int32, even.shape, 1)
    packet = jnp.where(lane < LOW, even, pltpu.roll(odd, LOW, 1))
    mine = jnp.full((8, LANES), owner[0, 0], jnp.int32).astype(F32)
    for peer in range(packets.shape[0]):
        packets[peer, pl.ds(0, SUM_ROWS)] = packet
        packets[peer, pl.ds(SUM_ROWS, 8)] = mine
    for x in range(nx):
        leave(x).wait()


def swapped(value, bit):
    row = lax.broadcasted_iota(jnp.int32, value.shape, 0)
    after = pltpu.roll(value, GROUP - bit, 0)
    before = pltpu.roll(value, bit, 0)
    return jnp.where((row & bit) == 0, after, before)


def coarse_kernel(place, arrived, out, levels):
    peers, rows, _ = arrived.shape
    flat = arrived.reshape(peers * rows, LANES)
    owner = flat[pl.ds(rows - 8, peers, stride=rows)]
    lane = lax.broadcasted_iota(jnp.int32, owner.shape, 1)
    base = place[0] - place[0] % GROUP
    chosen = jnp.where(owner == (base + lane).astype(F32), 1.0, 0.0)[:, :GROUP]
    blocks = []
    for r in range(SUM_ROWS):
        blocks.append(flat[pl.ds(r, peers, stride=rows)])
    gathered = jnp.concatenate(blocks, axis=1)
    owned = lax.dot_general(
        chosen, gathered, (((0,), (0,)), ((), ())),
        precision=lax.Precision.HIGHEST, preferred_element_type=F32,
    )
    resid = [owned[:, c * NAGG : (c + 1) * NAGG] for c in range(COMP)]
    diag = 1.0 + owned[:, COMP * NAGG :]
    at = lax.broadcasted_iota(jnp.int32, diag.shape, 1)
    for level in range(MERGES + 1):
        coupling = 0.2 * jnp.minimum(diag, pltpu.roll(diag, NAGG - 1, 1))
        coupling = jnp.where(at == NAGG - 1, 0.0, coupling)

        def apply(vector):
            upper = coupling * pltpu.roll(vector, NAGG - 1, 1)
            lower = pltpu.roll(coupling * vector, 1, 1)
            return diag * vector - (upper + lower)

        left = []
        for c in range(COMP):
            correction = 0.8 * resid[c] / diag
            correction = correction + 0.8 * (resid[c] - apply(correction)) / diag
            levels[level, c] = correction
            out[c, pl.ds(level, 1)] = levels[level, c, pl.ds(place[0] % GROUP, 1)]
            if level < MERGES:
                rest = resid[c] - apply(correction)
                left.append(rest + swapped(rest, 2**level))
        if level < MERGES:
            resid = left
            diag = diag + swapped(diag, 2**level)


def shift(axis, value, by):
    count = lax.axis_size(axis)
    pairs = [(i, i + by) for i in range(count) if 0 <= i + by < count]
    return lax.ppermute(value, axis, pairs)


def shards(right_side, viscosity, reaction, agg_ids, owner_map):
    nx, ny, nz = viscosity.shape
    nc = nz // LANES
    width = lax.axis_size("gx")
    place = lax.axis_index("gx").astype(jnp.int32).reshape(1)
    smem = pl.BlockSpec(memory_space=pltpu.SMEM)
    vmem = pl.BlockSpec(memory_space=pltpu.VMEM)
    small = pltpu.CompilerParams(vmem_limit_bytes=SMALL)

    def face(at_high):
        first = jnp.where(at_high, nx - WIDE, 0)
        first_v = jnp.where(at_high, nx - VWIDE, 0)
        return jnp.concatenate(
            [
                lax.dynamic_slice_in_dim(right_side, first, WIDE, axis=1).reshape(-1, ny, nz),
                lax.dynamic_slice_in_dim(viscosity, first_v, VWIDE, axis=0),
                lax.dynamic_slice_in_dim(reaction, first, WIDE, axis=0),
            ],
            axis=0,
        )

    even = place[0] % 2 == 0
    to_far, to_near = face(jnp.logical_not(even)), face(even)
    beyond = [(i, i - 1 if i % 2 == 0 else i + 1) for i in range(width)]
    beyond = [(i, k) for i, k in beyond if 0 <= k < width]
    far = lax.ppermute(to_far, "gx", beyond)
    near = lax.ppermute(to_near, "gx", [(i, i ^ 1) for i in range(width)])
    y_message = jax.ShapeDtypeStruct((nx * Y_ROWS, nz), F32)
    to_y_low, to_y_high = pl.pallas_call(
        pack_y,
        out_shape=(y_message, y_message),
        compiler_params=small,
        name="pack_y",
    )(right_side, viscosity, reaction)
    y_low = shift("gy", to_y_high, 1)
    y_high = shift("gy", to_y_low, -1)
    corner = jax.ShapeDtypeStruct((40, nz), F32)
    to_c_low, to_c_high = pl.pallas_call(
        pack_corners,
        out_shape=(corner, corner),
        in_specs=[smem, vmem, vmem],
        compiler_params=small,
        name="pack_corners",
    )(place, near, far)
    c_low = shift("gy", to_c_high, 1)
    c_high = shift("gy", to_c_low, -1)

    wide = (nx + 2 * X0, nc, ny + 2 * Y0, LANES)
    velocity, packets = pl.pallas_call(
        fine_kernel,
        out_shape=(
            jax.ShapeDtypeStruct(right_side.shape, F32),
            jax.ShapeDtypeStruct((width, SUM_ROWS + 8, LANES), F32),
        ),
        in_specs=[smem, smem] + [vmem] * 10,
        out_specs=(pl.BlockSpec(memory_space=pl.ANY), vmem),
        scratch_shapes=[
            pltpu.VMEM(wide, F32),
            pltpu.VMEM(wide, F32),
            pltpu.VMEM((COMP,) + wide, F32),
            pltpu.VMEM(wide, F32),
            pltpu.VMEM((COMP,) + wide, F32),
            pltpu.VMEM((COMP,) + wide, F32),
            pltpu.VMEM(wide, F32),
            pltpu.VMEM((2 * (COMP + 1),) + wide[1:], F32),
            pltpu.VMEM((nc, ny, LANES), F32),
            pltpu.VMEM((nc, ny, LANES), jnp.int32),
            pltpu.VMEM((2 * SUM_ROWS, LANES), F32),
            pltpu.VMEM(right_side.shape, F32),
            pltpu.SemaphoreType.DMA((nx,)),
        ],
        compiler_params=pltpu.CompilerParams(vmem_limit_bytes=BIG),
        name="fine",
    )(
        place, owner_map, right_side, viscosity, reaction, agg_ids,
        near, far, y_low, y_high, c_low, c_high,
    )
    arrived = lax.all_to_all(packets, "gx", 0, 0, tiled=True)
    corrections = pl.pallas_call(
        coarse_kernel,
        out_shape=jax.ShapeDtypeStruct((COMP, MERGES + 1, NAGG), F32),
        in_specs=[smem, vmem],
        scratch_shapes=[pltpu.VMEM((MERGES + 1, COMP, GROUP, NAGG), F32)],
        compiler_params=small,
        name="coarse",
    )(place, arrived)
    return (velocity, corrections.transpose(1, 0, 2)[None, None])


def solution(mesh):
    return jax.shard_map(
        shards,
        mesh=mesh,
        in_specs=(
            P(None, "gx", "gy", None),
            P("gx", "gy", None),
            P("gx", "gy", None),
            P("gx", "gy", None),
            P("gx", "gy"),
        ),
        out_specs=(P(None, "gx", "gy", None), P("gx", "gy", None, None, None)),
        check_vma=False,
    )
```

```python
import functools

import jax
import jax.numpy as jnp
from jax import lax
from jax.experimental import pallas as pl
from jax.experimental.pallas import tpu as pltpu
from jax.sharding import PartitionSpec as P

COMP = 3
NAGG = 512
MERGES = 3
GROUP = 2**MERGES
LANES = 128
WIDE = 3
VWIDE = WIDE + 1
VISC_AT = COMP * WIDE
REACT_AT = VISC_AT + VWIDE
ROWS = REACT_AT + WIDE
Y_VISC_AT = COMP * WIDE
Y_REACT_AT = Y_VISC_AT + WIDE
Y_ROWS = Y_REACT_AT + WIDE
CORNER = 18
X0 = VWIDE
Y0 = VWIDE
F32 = jnp.float32
HIGH = 8
LOW = NAGG // HIGH
SUM_ROWS = (COMP + 1) * NAGG // LANES
BIG = 32 * 2**20
SMALL = 8 * 2**20


def corner_rows():
    table = []
    for away, at in ((1, 0), (2, 11), (3, 17)):
        left = WIDE - away
        if left:
            for c in range(COMP):
                table.append((away, "rhs", c, at, left))
                at += left
        table.append((away, "visc", 0, at, left + 1))
        at += left + 1
        if left:
            table.append((away, "react", 0, at, left))
    return table


def by_parity(place, act, *pairs):
    even = place[0] % 2 == 0

    @pl.when(even)
    def _():
        act(*[ref for first, second in pairs for ref in (second, first)])

    @pl.when(jnp.logical_not(even))
    def _():
        act(*[ref for pair in pairs for ref in pair])


def pack_y(place, rhs, visc, react, y_first, y_second):
    by_parity(place, functools.partial(gy_faces, rhs, visc, react), (y_first, y_second))


def gy_faces(rhs, visc, react, y_low, y_high):
    nx, ny, _ = visc.shape
    for x in range(nx):
        at = x * Y_ROWS
        for c in range(COMP):
            rows = pl.ds(at + c * WIDE, WIDE)
            y_low[rows] = rhs[c, x, pl.ds(0, WIDE)]
            y_high[rows] = rhs[c, x, pl.ds(ny - WIDE, WIDE)]
        rows = pl.ds(at + Y_VISC_AT, WIDE)
        y_low[rows] = visc[x, pl.ds(0, WIDE)]
        y_high[rows] = visc[x, pl.ds(ny - WIDE, WIDE)]
        at = at + Y_REACT_AT
        y_low[pl.ds(at, WIDE - 1)] = react[x, pl.ds(0, WIDE - 1)]
        last = react[x, pl.ds(WIDE - 1, 1)] + 0.5 * visc[x, pl.ds(WIDE, 1)]
        y_low[pl.ds(at + WIDE - 1, 1)] = last
        last = react[x, pl.ds(ny - WIDE, 1)] + 0.5 * visc[x, pl.ds(ny - WIDE - 1, 1)]
        y_high[pl.ds(at, 1)] = last
        y_high[pl.ds(at + 1, WIDE - 1)] = react[x, pl.ds(ny - WIDE + 1, WIDE - 1)]


def pack_corners(place, near, far, c_first, c_second):
    even = place[0] % 2 == 0
    ny = near.shape[1]

    def fill(c_low, c_high):
        for side, (source, at_high) in enumerate(((near, even), (far, jnp.logical_not(even)))):
            for away, kind, c, at, count in corner_rows():
                width = VWIDE if kind == "visc" else WIDE
                first = {"rhs": c * WIDE, "visc": VISC_AT, "react": REACT_AT}[kind]
                index = first + jnp.where(at_high, away - 1, width - away)
                rows = pl.ds(side * CORNER + at, count)
                c_low[rows] = source[index, pl.ds(0, count)]
                c_high[rows] = source[index, pl.ds(ny - count, count)]

    by_parity(place, fill, (c_first, c_second))


def chunks_of(value):
    return [value[..., c * LANES : (c + 1) * LANES] for c in range(value.shape[-1] // LANES)]


def z_up(parts):
    lane = lax.broadcasted_iota(jnp.int32, parts[0].shape, 1)
    turned = [pltpu.roll(p, LANES - 1, 1) for p in parts]
    turned.append(jnp.zeros_like(parts[0]))
    return [jnp.where(lane == LANES - 1, turned[i + 1], turned[i]) for i in range(len(parts))]


def z_down(parts):
    lane = lax.broadcasted_iota(jnp.int32, parts[0].shape, 1)
    turned = [jnp.zeros_like(parts[0])] + [pltpu.roll(p, 1, 1) for p in parts]
    return [jnp.where(lane == 0, turned[i], turned[i + 1]) for i in range(len(parts))]


def fine_kernel(
    place, owner, rhs, visc, react, ids, near, far, y_first, y_second, c_first, c_second,
    vel_out, packets,
    half_x, react_x, rhs_x, inv_x, vel_a, vel_b, diag_s, terms, low_s, high_s, sums, vel_s, sems,
):
    nx, ny, nz = visc.shape
    nc = nz // LANES

    def put(kind, c, x, rows, value):
        for i, part in enumerate(chunks_of(value)):
            if kind == "rhs":
                rhs_x[c, x, i, rows] = part
            elif kind == "visc":
                half_x[x, i, rows] = 0.5 * part
            else:
                react_x[x, i, rows] = part

    own = pl.ds(Y0, ny)

    nothing = jnp.zeros((1, nz), F32)
    for x in range(nx):
        for c in range(COMP):
            put("rhs", c, x + X0, own, rhs[c, x])
        put("visc", 0, x + X0, own, visc[x])
        put("visc", 0, x + X0, pl.ds(Y0 - VWIDE, 1), nothing)
        put("visc", 0, x + X0, pl.ds(Y0 + ny + WIDE, 1), nothing)
        put("react", 0, x + X0, own, react[x])
    even = place[0] % 2 == 0
    for source, at_high in ((near, even), (far, jnp.logical_not(even))):
        for away in range(1, VWIDE + 1):
            x = jnp.where(at_high, X0 + nx - 1 + away, X0 - away)
            place_v = jnp.where(at_high, away - 1, VWIDE - away)
            put("visc", 0, x, own, source[VISC_AT + place_v])
            if away <= WIDE:
                place_w = jnp.where(at_high, away - 1, WIDE - away)
                for c in range(COMP):
                    put("rhs", c, x, own, source[c * WIDE + place_w])
                put("react", 0, x, own, source[REACT_AT + place_w])

    def fill_y(y_high, y_low, c_high, c_low):
        before, after = pl.ds(Y0 - WIDE, WIDE), pl.ds(Y0 + ny, WIDE)
        for x in range(nx):
            at = x * Y_ROWS
            for c in range(COMP):
                rows = pl.ds(at + c * WIDE, WIDE)
                put("rhs", c, x + X0, before, y_low[rows])
                put("rhs", c, x + X0, after, y_high[rows])
            rows = pl.ds(at + Y_VISC_AT, WIDE)
            put("visc", 0, x + X0, before, y_low[rows])
            put("visc", 0, x + X0, after, y_high[rows])
            rows = pl.ds(at + Y_REACT_AT, WIDE)
            put("react", 0, x + X0, before, y_low[rows])
            put("react", 0, x + X0, after, y_high[rows])
        for side, at_high in enumerate((even, jnp.logical_not(even))):
            for away, kind, c, at, count in corner_rows():
                before, after = pl.ds(Y0 - count, count), pl.ds(Y0 + ny, count)
                x = jnp.where(at_high, X0 + nx - 1 + away, X0 - away)
                rows = pl.ds(side * CORNER + at, count)
                put(kind, c, x, before, c_low[rows])
                put(kind, c, x, after, c_high[rows])

    by_parity(place, fill_y, (y_first, y_second), (c_first, c_second))

    def y_up(value):
        return pltpu.roll(value, value.shape[0] - 1, 0)

    def y_down(value):
        return pltpu.roll(value, 1, 0)

    def prepare(x, carry):
        here = [half_x[x, i] for i in range(nc)]
        up = z_up(here)
        down = z_down(here)
        for i in range(nc):
            beside = half_x[x + 1, i] + half_x[x - 1, i]
            beside = beside + y_up(here[i]) + y_down(here[i])
            beside = beside + up[i] + down[i]
            mass = react_x[x, i]
            diag = mass + (6.0 * here[i] + beside)
            inv = jnp.where(mass > 0.0, 0.8 / diag, 0.0)
            diag_s[x, i] = diag
            inv_x[x, i] = inv
            for c in range(COMP):
                vel_a[c, x, i] = inv * rhs_x[c, x, i]
        return carry

    lax.fori_loop(X0 - WIDE, X0 + nx + WIDE, prepare, 0, unroll=True)

    def stencil(vel, x, emit):
        shape = half_x.shape[2:]
        lane = lax.broadcasted_iota(jnp.int32, shape, 1)
        is_first, is_last = lane == 0, lane == LANES - 1
        none = jnp.zeros(shape, F32)
        half = [half_x[x, i] for i in range(nc)]
        half_up = [pltpu.roll(h, LANES - 1, 1) for h in half] + [none]
        here = [[vel[c, x, i] for i in range(nc)] for c in range(COMP)]
        turned = [[pltpu.roll(h, LANES - 1, 1) for h in part] + [none] for part in here]
        last = [none] * COMP
        for i in range(nc):
            w_x = half[i] + half_x[x + 1, i]
            w_x_before = half[i] + half_x[x - 1, i]
            w_y = half[i] + y_up(half[i])
            w_z = half[i] + jnp.where(is_last, half_up[i + 1], half_up[i])
            for c in range(COMP):
                up = jnp.where(is_last, turned[c][i + 1], turned[c][i])
                down = pltpu.roll(w_z * here[c][i], 1, 1)
                total = w_x * vel[c, x + 1, i] + w_x_before * vel[c, x - 1, i]
                total = total + w_y * y_up(here[c][i]) + y_down(w_y * here[c][i])
                total = total + w_z * up + jnp.where(is_first, last[c], down)
                last[c] = down
                emit(c, i, here[c][i], total)

    def sweep(source, target, reach):
        def step(x, carry):
            def emit(c, i, here, beside):
                added = inv_x[x, i] * (rhs_x[c, x, i] + beside)
                target[c, x, i] = 0.2 * here + added

            stencil(source, x, emit)
            return carry

        lax.fori_loop(X0 - reach, X0 + nx + reach, step, 0, unroll=True)

    sweep(vel_a, vel_b, 2)
    sweep(vel_b, vel_a, 1)

    in_high = lax.broadcasted_iota(jnp.int32, (HIGH, LANES), 0)
    label = lax.broadcasted_iota(jnp.int32, (LOW, LANES), 0).astype(F32)
    label = label.astype(jnp.bfloat16).reshape(LOW // 16, 16, LANES)
    ones, zeros = jnp.ones_like(label), jnp.zeros_like(label)

    def leave(x):
        return pltpu.make_async_copy(vel_s.at[:, x], vel_out.at[:, x], sems.at[x])

    def gather(x, total):
        def split(t, i, value):
            top = value.astype(jnp.bfloat16).astype(F32)
            terms[2 * t, i] = top
            terms[2 * t + 1, i] = value - top

        def emit(c, i, here, beside):
            vel_s[c, x - X0, :, i * LANES : (i + 1) * LANES] = here[Y0 : Y0 + ny]
            split(c, i, rhs_x[c, x, i] - (diag_s[x, i] * here - beside))

        stencil(vel_a, x, emit)
        leave(x - X0).start()
        for i in range(nc):
            split(COMP, i, diag_s[x, i])
        for i in range(nc):
            ident = ids[x - X0, :, i * LANES : (i + 1) * LANES]
            low_s[i] = (ident % LOW).astype(F32)
            high_s[i] = ident // LOW
        for y in range(ny):
            left, right = [], []
            row, at = pl.ds(y, 1), pl.ds(Y0 + y, 1)
            for i in range(nc):
                mask = high_s[i, row] == in_high
                parts = [jnp.where(mask, terms[t, i, at], 0.0) for t in range(2 * (COMP + 1))]
                left.append(jnp.concatenate(parts, axis=0).astype(jnp.bfloat16))
                low = jnp.broadcast_to(low_s[i, row], (16, LANES)).astype(jnp.bfloat16)
                hot = jnp.where(low[None] == label, ones, zeros)
                right.append(hot.reshape(LOW, LANES))
            total = total + lax.dot_general(
                jnp.concatenate(left, axis=1),
                jnp.concatenate(right, axis=1),
                (((1,), (1,)), ((), ())),
                preferred_element_type=F32,
            )
        return total

    width = 2 * (COMP + 1) * HIGH
    total = lax.fori_loop(X0, X0 + nx, gather, jnp.zeros((width, LOW), F32), unroll=4)
    for t in range(COMP + 1):
        at = 2 * HIGH * t
        both = total[at : at + HIGH] + total[at + HIGH : at + 2 * HIGH]
        sums[pl.ds(HIGH * t, HIGH), pl.ds(0, LOW)] = both
    half = SUM_ROWS
    even = sums[pl.ds(0, half, stride=2)]
    odd = sums[pl.ds(1, half, stride=2)]
    lane = lax.broadcasted_iota(jnp.int32, even.shape, 1)
    packet = jnp.where(lane < LOW, even, pltpu.roll(odd, LOW, 1))
    mine = jnp.full((8, LANES), owner[0, 0], jnp.int32).astype(F32)
    for peer in range(packets.shape[0]):
        packets[peer, pl.ds(0, SUM_ROWS)] = packet
        packets[peer, pl.ds(SUM_ROWS, 8)] = mine
    for x in range(nx):
        leave(x).wait()


def swapped(value, bit):
    row = lax.broadcasted_iota(jnp.int32, value.shape, 0)
    after = pltpu.roll(value, GROUP - bit, 0)
    before = pltpu.roll(value, bit, 0)
    return jnp.where((row & bit) == 0, after, before)


def coarse_kernel(place, arrived, out, levels):
    peers, rows, _ = arrived.shape
    flat = arrived.reshape(peers * rows, LANES)
    owner = flat[pl.ds(rows - 8, peers, stride=rows)]
    lane = lax.broadcasted_iota(jnp.int32, owner.shape, 1)
    base = place[0] - place[0] % GROUP
    chosen = jnp.where(owner == (base + lane).astype(F32), 1.0, 0.0)[:, :GROUP]
    blocks = []
    for r in range(SUM_ROWS):
        blocks.append(flat[pl.ds(r, peers, stride=rows)])
    gathered = jnp.concatenate(blocks, axis=1)
    owned = lax.dot_general(
        chosen, gathered, (((0,), (0,)), ((), ())),
        precision=lax.Precision.HIGHEST, preferred_element_type=F32,
    )
    resid = [owned[:, c * NAGG : (c + 1) * NAGG] for c in range(COMP)]
    diag = 1.0 + owned[:, COMP * NAGG :]
    at = lax.broadcasted_iota(jnp.int32, diag.shape, 1)
    for level in range(MERGES + 1):
        coupling = 0.2 * jnp.minimum(diag, pltpu.roll(diag, NAGG - 1, 1))
        coupling = jnp.where(at == NAGG - 1, 0.0, coupling)

        def apply(vector):
            upper = coupling * pltpu.roll(vector, NAGG - 1, 1)
            lower = pltpu.roll(coupling * vector, 1, 1)
            return diag * vector - (upper + lower)

        left = []
        for c in range(COMP):
            correction = 0.8 * resid[c] / diag
            correction = correction + 0.8 * (resid[c] - apply(correction)) / diag
            levels[level, c] = correction
            out[c, pl.ds(level, 1)] = levels[level, c, pl.ds(place[0] % GROUP, 1)]
            if level < MERGES:
                rest = resid[c] - apply(correction)
                left.append(rest + swapped(rest, 2**level))
        if level < MERGES:
            resid = left
            diag = diag + swapped(diag, 2**level)


def shards(right_side, viscosity, reaction, agg_ids, owner_map):
    nx, ny, nz = viscosity.shape
    nc = nz // LANES
    width = lax.axis_size("gx")
    place = lax.axis_index("gx").astype(jnp.int32).reshape(1)
    smem = pl.BlockSpec(memory_space=pltpu.SMEM)
    vmem = pl.BlockSpec(memory_space=pltpu.VMEM)
    small = pltpu.CompilerParams(vmem_limit_bytes=SMALL)

    def face(at_high):
        first = jnp.where(at_high, nx - WIDE, 0)
        first_v = jnp.where(at_high, nx - VWIDE, 0)
        return jnp.concatenate(
            [
                lax.dynamic_slice_in_dim(right_side, first, WIDE, axis=1).reshape(-1, ny, nz),
                lax.dynamic_slice_in_dim(viscosity, first_v, VWIDE, axis=0),
                lax.dynamic_slice_in_dim(reaction, first, WIDE, axis=0),
            ],
            axis=0,
        )

    even = place[0] % 2 == 0
    to_far, to_near = face(jnp.logical_not(even)), face(even)
    beyond = [(i, i - 1 if i % 2 == 0 else i + 1) for i in range(width)]
    beyond = [(i, k) for i, k in beyond if 0 <= k < width]
    far = lax.ppermute(to_far, "gx", beyond)
    near = lax.ppermute(to_near, "gx", [(i, i ^ 1) for i in range(width)])
    y_message = jax.ShapeDtypeStruct((nx * Y_ROWS, nz), F32)
    to_first, to_second = pl.pallas_call(
        pack_y,
        out_shape=(y_message, y_message),
        in_specs=[smem, vmem, vmem, vmem],
        compiler_params=small,
        name="pack_y",
    )(place, right_side, viscosity, reaction)
    corner = jax.ShapeDtypeStruct((40, nz), F32)
    to_c_first, to_c_second = pl.pallas_call(
        pack_corners,
        out_shape=(corner, corner),
        in_specs=[smem, vmem, vmem],
        compiler_params=small,
        name="pack_corners",
    )(place, near, far)

    def along_gy(value, by):
        height = lax.axis_size("gy")
        pairs = []
        for i in range(width):
            for j in range(height):
                k = j + by if i % 2 == 0 else j - by
                if 0 <= k < height:
                    pairs.append((i * height + j, i * height + k))
        return lax.ppermute(value, ("gx", "gy"), pairs)

    y_first = along_gy(to_first, 1)
    y_second = along_gy(to_second, -1)
    c_first = along_gy(to_c_first, 1)
    c_second = along_gy(to_c_second, -1)

    wide = (nx + 2 * X0, nc, ny + 2 * Y0, LANES)
    velocity, packets = pl.pallas_call(
        fine_kernel,
        out_shape=(
            jax.ShapeDtypeStruct(right_side.shape, F32),
            jax.ShapeDtypeStruct((width, SUM_ROWS + 8, LANES), F32),
        ),
        in_specs=[smem, smem] + [vmem] * 10,
        out_specs=(pl.BlockSpec(memory_space=pl.ANY), vmem),
        scratch_shapes=[
            pltpu.VMEM(wide, F32),
            pltpu.VMEM(wide, F32),
            pltpu.VMEM((COMP,) + wide, F32),
            pltpu.VMEM(wide, F32),
            pltpu.VMEM((COMP,) + wide, F32),
            pltpu.VMEM((COMP,) + wide, F32),
            pltpu.VMEM(wide, F32),
            pltpu.VMEM((2 * (COMP + 1),) + wide[1:], F32),
            pltpu.VMEM((nc, ny, LANES), F32),
            pltpu.VMEM((nc, ny, LANES), jnp.int32),
            pltpu.VMEM((2 * SUM_ROWS, LANES), F32),
            pltpu.VMEM(right_side.shape, F32),
            pltpu.SemaphoreType.DMA((nx,)),
        ],
        compiler_params=pltpu.CompilerParams(vmem_limit_bytes=BIG),
        name="fine",
    )(
        place, owner_map, right_side, viscosity, reaction, agg_ids,
        near, far, y_first, y_second, c_first, c_second,
    )
    arrived = lax.all_to_all(packets, "gx", 0, 0, tiled=True)
    corrections = pl.pallas_call(
        coarse_kernel,
        out_shape=jax.ShapeDtypeStruct((COMP, MERGES + 1, NAGG), F32),
        in_specs=[smem, vmem],
        scratch_shapes=[pltpu.VMEM((MERGES + 1, COMP, GROUP, NAGG), F32)],
        compiler_params=small,
        name="coarse",
    )(place, arrived)
    return (velocity, corrections.transpose(1, 0, 2)[None, None])


def solution(mesh):
    return jax.shard_map(
        shards,
        mesh=mesh,
        in_specs=(
            P(None, "gx", "gy", None),
            P("gx", "gy", None),
            P("gx", "gy", None),
            P("gx", "gy", None),
            P("gx", "gy"),
        ),
        out_specs=(P(None, "gx", "gy", None), P("gx", "gy", None, None, None)),
        check_vma=False,
    )
```
